256 devices in a mesh: blk: 256 (over z, x, y, core).
Axes of the slice: x: 4, y: 4, z: 8, core: 2. Of those that a mesh axis runs over, the one named last changes fastest.
Arguments:
- embeddings: float32 [196608, 1024], P('blk')
- labels: int32 [196608], P('blk'), may hold values from 0 to 999
Outputs:
- agreement: float32 [196608], P('blk')
- log_weight: float32 [196608], P('blk')
The draws below stay inside these ranges and needn't reach their ends.
All inputs are finite; a program needn't handle non-finite values.
Results may differ from the reference program's by a relative error of at most 0.00087.
Values may be sent and summed in bfloat16 or wider, within the bound.
No kernel may reach another device: no remote copies, remote signals or barrier semaphores. Data moves between devices by JAX's collectives and lax.ppermute only.
A program may use at most 64 MiB of HBM per device.

```python
import jax
import jax.numpy as jnp
from jax import lax

D = 1024
CLASSES = 1000
ROWS = 768
STEPS = 4
TOTAL = 196608
N_BLK = 256


def shared_labels(key):
    drawn = jax.random.randint(key, (TOTAL,), 0, CLASSES, dtype=jnp.int32)
    return drawn.at[0].set(CLASSES - 1).at[1].set(0)


def draw_labels(key, part):
    return shared_labels(key)


def draw_embeddings(key, part):
    ids = shared_labels(key)
    key = jax.random.fold_in(key, 2)
    proto_key, flip_key, other_key, noise_key = jax.random.split(key, 4)
    protos = jax.random.normal(proto_key, (CLASSES, D), jnp.float32)
    flipped = jax.random.uniform(flip_key, (TOTAL,)) < 0.2
    others = jax.random.randint(other_key, (TOTAL,), 0, CLASSES, dtype=jnp.int32)
    source = jnp.where(flipped, others, ids)
    centre = protos[source] * 0.9
    values = centre + jax.random.normal(noise_key, (TOTAL, D), jnp.float32)
    return values.astype(jnp.float32)


def setup_inputs(seed: int = 0) -> dict:
    key_list = jax.random.split(jax.random.key(seed), 3)
    embeddings = draw_embeddings(jax.random.fold_in(key_list[2], 71), 0)
    labels = draw_labels(jax.random.fold_in(key_list[2], 71), 0)
    return dict(embeddings=embeddings, labels=labels)


tau_value = 0.1

def reference(embeddings, labels):
    unit = (embeddings / jnp.sqrt(lax.optimization_barrier(jnp.sum(embeddings * embeddings, axis=1, keepdims=True)) + 1e-06)).astype(jnp.bfloat16)
    blocks = unit.reshape(N_BLK, ROWS, D)
    block_ids = labels.reshape(N_BLK, ROWS)
    keep_self = 1.0 - jnp.eye(ROWS, dtype=jnp.float32)

    def one_block(index):
        mine = lax.dynamic_index_in_dim(blocks, index, 0, keepdims=False)
        mine_ids = lax.dynamic_index_in_dim(block_ids, index, 0, keepdims=False)
        same_sum = jnp.zeros((ROWS,), jnp.float32)
        total = jnp.zeros((ROWS,), jnp.float32)
        for offset in range(-STEPS, STEPS + 1):
            where = ((index + offset + N_BLK) % N_BLK).astype(jnp.int32)
            other = lax.dynamic_index_in_dim(blocks, where, 0, keepdims=False)
            other_ids = lax.dynamic_index_in_dim(block_ids, where, 0, keepdims=False)
            score = jnp.dot(mine, other.T, preferred_element_type=jnp.float32)
            weight = jnp.exp((score - 1.0) / tau_value)
            if offset == 0:
                weight = weight * keep_self
            match = (mine_ids[:, None] == other_ids[None, :]).astype(jnp.float32)
            same_sum = same_sum + lax.optimization_barrier(jnp.sum(weight * match, axis=1))
            total = total + lax.optimization_barrier(jnp.sum(weight, axis=1))
        return (same_sum, total)
    same_sum, total = lax.map(one_block, jnp.arange(N_BLK, dtype=jnp.int32))
    same_sum = same_sum.reshape(TOTAL)
    total = total.reshape(TOTAL)
    return (same_sum / total, jnp.log(total))
```

```python
import functools
import math

import jax
import jax.numpy as jnp
from jax import lax
from jax.experimental import pallas as pl
from jax.experimental.pallas import tpu as pltpu
from jax.sharding import PartitionSpec as P

TAU = 0.1
SCALE = math.log2(math.e) / TAU
HEAD = 16
LATE = 128
F32 = jnp.float32
BF16 = jnp.bfloat16


def vmem(count):
    return [pl.BlockSpec(memory_space=pltpu.VMEM)] * count


def call(kernel, out_shape, operands, name, tiles):
    return pl.pallas_call(
        kernel,
        out_shape=out_shape,
        in_specs=vmem(len(operands)),
        out_specs=jax.tree.map(lambda _: vmem(1)[0], out_shape),
        name=name,
        cost_estimate=pl.CostEstimate(
            flops=int(2 * tiles * 768 * 768 * 1024),
            bytes_accessed=sum(a.size * a.dtype.itemsize for a in operands),
            transcendentals=int(tiles * 768 * 768),
        ),
        compiler_params=pltpu.CompilerParams(vmem_limit_bytes=48 * 1024 * 1024),
    )(*operands)


def label_row(head):
    return (head[0:1, :] + head[1:2, :])


def label_column(head):
    ones = jnp.ones((HEAD, 128), BF16)
    return lax.dot_general(head, ones, (((0,), (0,)), ((), ())), preferred_element_type=F32)


def to_lanes(partial):
    ones = jnp.ones((8, 128), F32)
    return lax.dot_general(
        ones, partial, (((1,), (1,)), ((), ())), precision=lax.Precision.HIGHEST, preferred_element_type=F32
    )[0:1]


def tile(left, left_labels, right, right_labels, rows, columns, own=None):
    m, n = left.shape[0], right.shape[0]
    step = 256
    row_total = row_same = None
    totals, sames = [], []
    labels2 = jnp.concatenate([left_labels, left_labels], axis=1)
    for j in range(0, n, step):
        score = lax.dot_general(
            left, right[j : j + step], (((1,), (1,)), ((), ())), preferred_element_type=F32
        )
        weight = jnp.exp2(score * SCALE - SCALE)
        if own is not None:
            r = lax.broadcasted_iota(jnp.int32, (m, step), 0) + own
            c = lax.broadcasted_iota(jnp.int32, (m, step), 1) + j
            weight = jnp.where(r == c, 0.0, weight)
        same = jnp.where(labels2 == right_labels[:, j : j + step], weight, 0.0)
        if rows:
            a, b = weight[:, :128] + weight[:, 128:], same[:, :128] + same[:, 128:]
            row_total = a if row_total is None else row_total + a
            row_same = b if row_same is None else row_same + b
        if columns:
            totals.append(jnp.sum(weight, axis=0, keepdims=True))
            sames.append(jnp.sum(same, axis=0, keepdims=True))
    out = []
    if rows:
        out += [row_total, row_same]
    if columns:
        out += [jnp.concatenate(totals, axis=1), jnp.concatenate(sames, axis=1)]
    return out


def pair(left_ref, first, count, left_labels, right_ref, right_labels, rows, columns, own=False, row_start=0):
    right = right_ref[HEAD:, :]
    row_out, col = [], None
    step = min(384, count)
    for i in range(0, count, step):
        m = min(step, count - i)
        left = left_ref[first + i : first + i + m, :]
        got = tile(
            left, left_labels[row_start + i : row_start + i + m], right, right_labels, rows, columns,
            own=i if own else None,
        )
        if rows:
            row_out.append(jnp.concatenate([to_lanes(got[0]), to_lanes(got[1])], axis=0))
        if columns:
            both = jnp.concatenate(got[-2:], axis=0)
            col = both if col is None else col + both
    out = []
    if rows:
        out.append(jnp.concatenate(row_out, axis=1))
    if columns:
        out.append(col)
    return out if len(out) > 1 else out[0]


def norm_kernel(x_ref, labels_ref, out_ref):
    rows = x_ref.shape[0]
    for i in range(0, rows, 128):
        x = x_ref[i : i + 128, :]
        scale = lax.rsqrt(jnp.sum(x * x, axis=1, keepdims=True) + 1e-06)
        out_ref[HEAD + i : HEAD + i + 128, :] = (x * scale).astype(BF16)
    labels = labels_ref[...]
    low = lax.rem(labels, 256)
    wide = jnp.concatenate([labels - low, low], axis=0).astype(F32)
    wide = jnp.concatenate([wide, jnp.zeros((HEAD - 2, rows), F32)], axis=0)
    wide = jnp.concatenate([wide, jnp.zeros((HEAD, x_ref.shape[1] - rows), F32)], axis=1)
    out_ref[0:HEAD, :] = wide.astype(BF16)


def head_of(ref, rows):
    return ref[0:HEAD, 0:rows]


def first_kernel(u_ref, x_ref, own_ref, early_ref, late_ref):
    rows = u_ref.shape[0] - HEAD
    cut = u_ref.shape[0] - LATE
    early_ref[...] = u_ref[0:cut, :]
    late_ref[...] = u_ref[cut:, :]
    own_row = label_row(head_of(u_ref, rows).astype(F32))
    own_column = label_column(head_of(u_ref, rows))
    x_column = label_column(head_of(x_ref, rows))
    inside = pair(u_ref, HEAD, rows, own_column, u_ref, own_row, False, True, own=True)
    other = pair(x_ref, HEAD, rows, x_column, u_ref, own_row, False, True)
    own_ref[...] = inside + other


def second_kernel(u_ref, x_ref, a_ref, own_in_ref, own_ref, a_sum_ref):
    rows = u_ref.shape[0] - HEAD
    a_row = label_row(head_of(a_ref, rows).astype(F32))
    own_column = label_column(head_of(u_ref, rows))
    x_column = label_column(head_of(x_ref, rows))
    own_sum, a_sum = pair(u_ref, HEAD, rows, own_column, a_ref, a_row, True, True)
    a_sum2 = pair(x_ref, HEAD, rows, x_column, a_ref, a_row, False, True)
    own_ref[...] = own_in_ref[...] + own_sum
    a_sum_ref[...] = a_sum + a_sum2


def third_kernel(f_ref, a_ref, a_in_ref, a_sum_ref):
    rows = a_ref.shape[0] - HEAD
    a_row = label_row(head_of(a_ref, rows).astype(F32))
    f_column = label_column(head_of(f_ref, rows))
    a_sum_ref[...] = a_in_ref[...] + pair(f_ref, HEAD, rows, f_column, a_ref, a_row, False, True)


def fourth_kernel(first, count, skip, b_ref, head_ref, a_ref, x_ref, a_in_ref, a_sum_ref, b_sum_ref):
    rows = a_ref.shape[0] - HEAD
    a_row = label_row(head_of(a_ref, rows).astype(F32))
    x_row = label_row(head_of(x_ref, rows).astype(F32))
    b_column = label_column(head_of(head_ref, rows))
    b_sum, a_sum = pair(b_ref, skip, count, b_column, a_ref, a_row, True, True, row_start=first)
    b_sum2 = pair(b_ref, skip, count, b_column, x_ref, x_row, True, False, row_start=first)
    a_sum_ref[...] = a_in_ref[...] + a_sum
    b_sum_ref[...] = b_sum + b_sum2


def on_device(embeddings, labels):
    rows, depth = embeddings.shape
    n = lax.axis_size("blk")
    up = [(i, (i + 2) % n if i % 2 else (i - 2) % n) for i in range(n)]
    down = [(i, (i - 2) % n if i % 2 else (i + 2) % n) for i in range(n)]
    swap = [(i, i ^ 1) for i in range(n)]
    back = lambda route: [(d, s) for s, d in route]
    send = lambda array, route: lax.ppermute(array, "blk", route)
    struct = jax.ShapeDtypeStruct
    sums = struct((2, rows), F32)

    u = call(norm_kernel, struct((rows + HEAD, depth), BF16), (embeddings, labels[None, :]), "unit", 0.1)
    a = send(u, up)
    x = send(u, swap)
    early, late = struct((rows + HEAD - LATE, depth), BF16), struct((LATE, depth), BF16)
    own, early, late = call(first_kernel, (sums, early, late), (u, x), "own_and_partner", 2)
    b_early = send(early, down)
    b_late = send(late, down)
    f = send(a, swap)
    own, a_sum = call(second_kernel, (sums, sums), (u, x, a, own), "with_a", 2)
    a_sum = call(third_kernel, sums, (f, a, a_sum), "a_with_f", 1)
    a_sum, b_sum1 = call(
        functools.partial(fourth_kernel, 0, rows - LATE, HEAD),
        (sums, struct((2, rows - LATE), F32)),
        (b_early, b_early, a, x, a_sum),
        "with_b_early",
        1.7,
    )
    a_sum, b_sum2 = call(
        functools.partial(fourth_kernel, rows - LATE, LATE, 0),
        (sums, struct((2, LATE), F32)),
        (b_late, b_early[0:HEAD], a, x, a_sum),
        "with_b_late",
        0.3,
    )
    b_sum = jnp.concatenate([b_sum1, b_sum2], axis=1)
    from_a = send(a_sum, back(up))
    from_b = send(b_sum, back(down))
    total, same = own + from_a + from_b
    return same / total, jnp.log(total)


def solution(mesh):
    return jax.shard_map(
        on_device,
        mesh=mesh,
        in_specs=(P("blk", None), P("blk")),
        out_specs=(P("blk"), P("blk")),
        check_vma=False,
    )
```

```python
import functools
import math

import jax
import jax.numpy as jnp
from jax import lax
from jax.experimental import pallas as pl
from jax.experimental.pallas import tpu as pltpu
from jax.sharding import PartitionSpec as P

TAU = 0.1
SCALE = math.log2(math.e) / TAU
LANES = 128
HEAD = 16
EARLY = 512
LATE = 256
CHUNK = 512
STEP = 256
F32 = jnp.float32
BF16 = jnp.bfloat16


def call(kernel, out_shape, operands, name, tiles, in_specs=None, scratch=(), limit=48):
    vmem = pl.BlockSpec(memory_space=pltpu.VMEM)
    return pl.pallas_call(
        kernel,
        out_shape=out_shape,
        in_specs=in_specs or [vmem] * len(operands),
        out_specs=jax.tree.map(lambda _: vmem, out_shape),
        scratch_shapes=scratch,
        name=name,
        cost_estimate=pl.CostEstimate(
            flops=int(1.2e10 * tiles),
            bytes_accessed=1024,
            transcendentals=0,
        ),
        compiler_params=pltpu.CompilerParams(vmem_limit_bytes=limit * 1024 * 1024),
    )(*operands)


def images(ref, n, first, count, head=HEAD):
    slabs = (ref.shape[0] - head) // n
    return jnp.concatenate(
        [ref[head + k * n + first : head + k * n + first + count, :] for k in range(slabs)], axis=1
    )


def label_row(ref, n):
    head = ref[0:HEAD, :].astype(F32)
    groups = n // LANES
    return jnp.concatenate([head[k : k + 1] + head[k + groups : k + groups + 1] for k in range(groups)], axis=1)


def label_column(ref, n):
    groups = n // LANES
    row = lax.broadcasted_iota(jnp.int32, (HEAD, n), 0)
    group = lax.broadcasted_iota(jnp.int32, (HEAD, n), 1) // LANES
    pick = jnp.where((row == group) | (row == group + groups), 1.0, 0.0).astype(BF16)
    spread = lax.dot_general(ref[0:HEAD, :], pick, (((0,), (0,)), ((), ())), preferred_element_type=F32)
    return jnp.concatenate([spread[:, k * LANES : (k + 1) * LANES] for k in range(groups)], axis=0)


def along_lanes(partial):
    return jnp.concatenate(
        [
            jnp.sum(partial[i : i + LANES].T, axis=0, keepdims=True)
            for i in range(0, partial.shape[0], LANES)
        ],
        axis=1,
    )


def weigh(left, left_labels, right, right_labels, rows, columns, own=None):
    m, n = left.shape[0], right.shape[0]
    row_parts, column = [], None
    for i in range(0, m, CHUNK):
        chunk = min(CHUNK, m - i)
        here = left[i : i + chunk]
        labels = jnp.concatenate([left_labels[i : i + chunk]] * (STEP // LANES), axis=1)
        totals, sames, row_total, row_same = [], [], None, None
        for j in range(0, n, STEP):
            score = lax.dot_general(
                here, right[j : j + STEP], (((1,), (1,)), ((), ())), preferred_element_type=F32
            )
            weight = jnp.exp2(score * SCALE)
            if own is not None:
                r = lax.broadcasted_iota(jnp.int32, (chunk, STEP), 0) + (own + i)
                c = lax.broadcasted_iota(jnp.int32, (chunk, STEP), 1) + j
                weight = jnp.where(r == c, 0.0, weight)
            same = jnp.where(labels == right_labels[:, j : j + STEP], weight, 0.0)
            if rows:
                for k in range(0, STEP, LANES):
                    a, b = weight[:, k : k + LANES], same[:, k : k + LANES]
                    row_total = a if row_total is None else row_total + a
                    row_same = b if row_same is None else row_same + b
            if columns:
                totals.append(jnp.sum(weight, axis=0, keepdims=True))
                sames.append(jnp.sum(same, axis=0, keepdims=True))
        if rows:
            row_parts.append((row_total, row_same))
        if columns:
            both = jnp.concatenate([jnp.concatenate(totals, axis=1), jnp.concatenate(sames, axis=1)], axis=0)
            column = both if column is None else column + both
    rows_out = tuple(jnp.concatenate(p, axis=0) for p in zip(*row_parts)) if rows else None
    return rows_out, column


def add(*pairs):
    total, same = pairs[0]
    for more_total, more_same in pairs[1:]:
        total, same = total + more_total, same + more_same
    return jnp.concatenate([along_lanes(total), along_lanes(same)], axis=0)


def early_part(ref):
    return images(ref, EARLY, 0, EARLY)


def late_part(ref):
    return images(ref, LATE, 0, LATE, head=0)


def columns_of(early_ref, late):
    column = label_column(early_ref, EARLY + LATE)
    return column[EARLY:] if late else column[:EARLY]


def row_of(early_ref, late):
    row = label_row(early_ref, EARLY + LATE)
    return row[:, EARLY:] if late else row[:, :EARLY]


def unit_kernel(x_ref, labels_hbm, early_ref, late_ref, held, labels_ref, sems):
    n, depth = x_ref.shape
    parts = sems.shape[0] - 1
    part = n // parts
    copies = [
        pltpu.make_async_copy(x_ref.at[pl.ds(i * part, part), :], held.at[pl.ds(i * part, part), :], sems.at[i])
        for i in range(parts)
    ]
    labels_copy = pltpu.make_async_copy(labels_hbm, labels_ref, sems.at[parts])
    labels_copy.start()
    for copy in copies:
        copy.start()
    labels_copy.wait()
    labels = labels_ref[...]
    low = lax.rem(labels, 256)
    blank = jnp.zeros((HEAD - 2 * labels.shape[0], LANES), F32)
    head = jnp.concatenate([(labels - low).astype(F32), low.astype(F32), blank], axis=0)
    early_ref[0:HEAD, :] = head.astype(BF16)
    for i in range(parts):
        copies[i].wait()
        for q in range(i * part, (i + 1) * part, 64):
            x = held[q : q + 64, :]
            unit = (x * lax.rsqrt(jnp.sum(x * x, axis=1, keepdims=True) + 1e-06)).astype(BF16)
            for k in range(depth // LANES):
                slab = unit[:, k * LANES : (k + 1) * LANES]
                if q < EARLY:
                    early_ref[HEAD + k * EARLY + q : HEAD + k * EARLY + q + 64, :] = slab
                else:
                    late_ref[k * LATE + q - EARLY : k * LATE + q - EARLY + 64, :] = slab


def own_kernel(ue_ref, ul_ref, own_ref, copy_ref):
    copy_ref[...] = ul_ref[...]
    unit = jnp.concatenate([early_part(ue_ref), late_part(ul_ref)], axis=0)
    labels = label_row(ue_ref, EARLY + LATE)
    _, own = weigh(unit, label_column(ue_ref, EARLY + LATE), unit, labels, False, True, own=0)
    own_ref[...] = own


def partner_kernel(ue_ref, ul_ref, xe_ref, xl_ref, own_in_ref, own_ref):
    unit = jnp.concatenate([early_part(ue_ref), late_part(ul_ref)], axis=0)
    labels = label_row(ue_ref, EARLY + LATE)
    _, a = weigh(early_part(xe_ref), columns_of(xe_ref, False), unit, labels, False, True)
    _, b = weigh(late_part(xl_ref), columns_of(xe_ref, True), unit, labels, False, True)
    own_ref[...] = own_in_ref[...] + a + b


def is_even():
    return lax.rem(lax.axis_index("blk"), 2) == 0


def pick_kernel(p_ref, n_ref, after_ref, out_ref):
    even = is_even()

    @pl.when(even)
    def _():
        out_ref[...] = n_ref[...]

    @pl.when(jnp.logical_not(even))
    def _():
        out_ref[...] = p_ref[...]


def early_kernel(ue_ref, ul_ref, xe_ref, xl_ref, pe_ref, ne_ref, own_in_ref, own_ref, p_ref, n_ref):
    n, labels = early_part(ne_ref), columns_of(ne_ref, False)
    n1, own1 = weigh(n, labels, early_part(ue_ref), row_of(ue_ref, False), True, True)
    n2, own2 = weigh(n, labels, late_part(ul_ref), row_of(ue_ref, True), True, True)
    n3, _ = weigh(n, labels, early_part(xe_ref), row_of(xe_ref, False), True, False)
    n4, _ = weigh(n, labels, late_part(xl_ref), row_of(xe_ref, True), True, False)
    n5, p1 = weigh(n, labels, early_part(pe_ref), row_of(pe_ref, False), True, True)
    n_ref[...] = add(n1, n2, n3, n4, n5)
    own_ref[:, :EARLY] = own_in_ref[:, :EARLY] + own1
    own_ref[:, EARLY:] = own_in_ref[:, EARLY:] + own2
    p, labels = early_part(pe_ref), row_of(pe_ref, False)
    _, p2 = weigh(early_part(xe_ref), columns_of(xe_ref, False), p, labels, False, True)
    _, p3 = weigh(late_part(xl_ref), columns_of(xe_ref, True), p, labels, False, True)
    p_ref[...] = p1 + p2 + p3


def early_f_kernel(fe_ref, pe_ref, ne_ref, p_in_ref, n_in_ref, p_ref, n_ref):
    even = is_even()
    right = jnp.where(even, early_part(ne_ref), early_part(pe_ref))
    labels = jnp.where(even, row_of(ne_ref, False), row_of(pe_ref, False))
    _, more = weigh(early_part(fe_ref), columns_of(fe_ref, False), right, labels, False, True)
    p_ref[...] = p_in_ref[...] + jnp.where(even, 0.0, more)
    n_ref[...] = n_in_ref[...] + jnp.where(even, more, 0.0)


def late_kernel(
    ue_ref, ul_ref, xe_ref, xl_ref, pe_ref, ne_ref, pl_ref, nl_ref, own_in_ref, p_in_ref, n_in_ref,
    own_ref, p_ref, n_ref,
):
    n, labels = late_part(nl_ref), columns_of(ne_ref, True)
    n1, own1 = weigh(n, labels, early_part(ue_ref), row_of(ue_ref, False), True, True)
    n2, own2 = weigh(n, labels, late_part(ul_ref), row_of(ue_ref, True), True, True)
    n3, _ = weigh(n, labels, early_part(xe_ref), row_of(xe_ref, False), True, False)
    n4, _ = weigh(n, labels, late_part(xl_ref), row_of(xe_ref, True), True, False)
    n5, p1 = weigh(n, labels, early_part(pe_ref), row_of(pe_ref, False), True, True)
    n6, p2 = weigh(n, labels, late_part(pl_ref), row_of(pe_ref, True), True, True)
    p, labels = late_part(pl_ref), columns_of(pe_ref, True)
    p3, n7 = weigh(p, labels, early_part(ne_ref), row_of(ne_ref, False), True, True)
    p4, _ = weigh(p, labels, early_part(xe_ref), row_of(xe_ref, False), True, False)
    p5, _ = weigh(p, labels, late_part(xl_ref), row_of(xe_ref, True), True, False)
    own_ref[:, :EARLY] = own_in_ref[:, :EARLY] + own1
    own_ref[:, EARLY:] = own_in_ref[:, EARLY:] + own2
    n_ref[:, :EARLY] = n_in_ref[...] + n7
    n_ref[:, EARLY:] = add(n1, n2, n3, n4, n5, n6)
    p_ref[:, :EARLY] = p_in_ref[...] + p1
    p_ref[:, EARLY:] = p2 + add(p3, p4, p5)


def late_f_kernel(fe_ref, fl_ref, pe_ref, ne_ref, pl_ref, nl_ref, p_in_ref, n_in_ref, p_ref, n_ref):
    even = is_even()
    right = jnp.where(even, early_part(ne_ref), early_part(pe_ref))
    late = jnp.where(even, late_part(nl_ref), late_part(pl_ref))
    labels = jnp.where(even, row_of(ne_ref, False), row_of(pe_ref, False))
    late_labels = jnp.where(even, row_of(ne_ref, True), row_of(pe_ref, True))
    f, f_labels = late_part(fl_ref), columns_of(fe_ref, True)
    _, a = weigh(f, f_labels, right, labels, False, True)
    _, b = weigh(f, f_labels, late, late_labels, False, True)
    _, c = weigh(early_part(fe_ref), columns_of(fe_ref, False), late, late_labels, False, True)
    more = jnp.concatenate([a, b + c], axis=1)
    p_ref[...] = p_in_ref[...] + jnp.where(even, 0.0, more)
    n_ref[...] = n_in_ref[...] + jnp.where(even, more, 0.0)


def last_kernel(own_ref, a_ref, b_ref, agreement_ref, log_ref):
    sums = own_ref[...] + a_ref[...] + b_ref[...]
    agreement = sums[1:2] / sums[0:1]
    log_weight = jnp.log(sums[0:1]) - 1.0 / TAU
    for k in range(agreement_ref.shape[0]):
        agreement_ref[k : k + 1, :] = agreement[:, k * LANES : (k + 1) * LANES]
        log_ref[k : k + 1, :] = log_weight[:, k * LANES : (k + 1) * LANES]


def on_device(embeddings, labels):
    n, depth = embeddings.shape
    slabs = depth // LANES
    size = lax.axis_size("blk")
    up = [(i, (i + 2) % size) for i in range(size)]
    down = [(i, (i - 2) % size) for i in range(size)]
    swap = [(i, i ^ 1) for i in range(size)]
    send = lambda array, route: lax.ppermute(array, "blk", route)
    struct = jax.ShapeDtypeStruct
    sums, early_sums = struct((2, n), F32), struct((2, EARLY), F32)
    early, late = struct((HEAD + slabs * EARLY, LANES), BF16), struct((slabs * LATE, LANES), BF16)

    ue, ul = call(
        unit_kernel,
        (early, late),
        (embeddings, labels.reshape(n // LANES, LANES)),
        "unit",
        0.1,
        in_specs=[pl.BlockSpec(memory_space=pl.ANY)] * 2,
        scratch=[
            pltpu.VMEM((n, depth), F32),
            pltpu.VMEM((n // LANES, LANES), jnp.int32),
            pltpu.SemaphoreType.DMA((7,)),
        ],
        limit=52,
    )
    pe = send(ue, up)
    ne = send(ue, down)
    xe = send(ue, swap)
    xl = send(ul, swap)
    own, copy = call(own_kernel, (sums, late), (ue, ul), "own", 1)
    late_p = send(copy, up)
    late_n = send(copy, down)
    own = call(partner_kernel, sums, (ue, ul, xe, xl, own), "with_partner", 1)

    fe = send(call(pick_kernel, early, (pe, ne, own), "pick", 0.1), swap)
    own, p, q = call(
        early_kernel, (sums, early_sums, early_sums), (ue, ul, xe, xl, pe, ne, own), "early", 2.5
    )
    p, q = call(early_f_kernel, (early_sums, early_sums), (fe, pe, ne, p, q), "early_f", 0.5)
    fl = send(call(pick_kernel, late, (late_p, late_n, p), "pick_late", 0.1), swap)
    own, p, q = call(
        late_kernel, (sums, sums, sums), (ue, ul, xe, xl, pe, ne, late_p, late_n, own, p, q), "late", 1.5
    )
    p, q = call(late_f_kernel, (sums, sums), (fe, fl, pe, ne, late_p, late_n, p, q), "late_f", 0.6)
    from_lower = send(q, up)
    from_upper = send(p, down)
    shape = struct((n // LANES, LANES), F32)
    agreement, log_weight = call(last_kernel, (shape, shape), (own, from_lower, from_upper), "last", 0.01)
    return agreement.reshape(n), log_weight.reshape(n)


def solution(mesh):
    return jax.shard_map(
        on_device,
        mesh=mesh,
        in_specs=(P("blk", None), P("blk")),
        out_specs=(P("blk"), P("blk")),
        check_vma=False,
    )
```

```python
import functools
import math

import jax
import jax.numpy as jnp
from jax import lax
from jax.experimental import pallas as pl
from jax.experimental.pallas import tpu as pltpu
from jax.sharding import PartitionSpec as P

TAU = 0.1
SCALE = math.log2(math.e) / TAU
LANES = 128
HEAD = 16
EARLY = 512
LATE = 256
CHUNK = 512
STEP = 256
F32 = jnp.float32
BF16 = jnp.bfloat16


def call(kernel, out_shape, operands, name, tiles, in_specs=None, scratch=(), limit=28):
    vmem = pl.BlockSpec(memory_space=pltpu.VMEM)
    return pl.pallas_call(
        kernel,
        out_shape=out_shape,
        in_specs=in_specs or [vmem] * len(operands),
        out_specs=jax.tree.map(lambda _: vmem, out_shape),
        scratch_shapes=scratch,
        name=name,
        cost_estimate=pl.CostEstimate(
            flops=int(1.2e10 * tiles),
            bytes_accessed=1024,
            transcendentals=0,
        ),
        compiler_params=pltpu.CompilerParams(vmem_limit_bytes=limit * 1024 * 1024),
    )(*operands)


def images(ref, n, first, count, head=HEAD):
    slabs = (ref.shape[0] - head) // n
    return jnp.concatenate(
        [ref[head + k * n + first : head + k * n + first + count, :] for k in range(slabs)], axis=1
    )


def label_row(ref, n):
    head = ref[0:HEAD, :].astype(F32)
    groups = n // LANES
    return jnp.concatenate([head[k : k + 1] + head[k + groups : k + groups + 1] for k in range(groups)], axis=1)


def label_column(ref, n):
    groups = n // LANES
    row = lax.broadcasted_iota(jnp.int32, (HEAD, n), 0)
    group = lax.broadcasted_iota(jnp.int32, (HEAD, n), 1) // LANES
    pick = jnp.where((row == group) | (row == group + groups), 1.0, 0.0).astype(BF16)
    spread = lax.dot_general(ref[0:HEAD, :], pick, (((0,), (0,)), ((), ())), preferred_element_type=F32)
    return jnp.concatenate([spread[:, k * LANES : (k + 1) * LANES] for k in range(groups)], axis=0)


def along_lanes(partial):
    return jnp.concatenate(
        [
            jnp.sum(partial[i : i + LANES].T, axis=0, keepdims=True)
            for i in range(0, partial.shape[0], LANES)
        ],
        axis=1,
    )


def weigh(left, left_labels, right, right_labels, rows, columns, own=None):
    m, n = left.shape[0], right.shape[0]
    row_parts, column = [], None
    for i in range(0, m, CHUNK):
        chunk = min(CHUNK, m - i)
        here = left[i : i + chunk]
        labels = jnp.concatenate([left_labels[i : i + chunk]] * (STEP // LANES), axis=1)
        totals, sames, row_total, row_same = [], [], None, None
        for j in range(0, n, STEP):
            score = lax.dot_general(
                here, right[j : j + STEP], (((1,), (1,)), ((), ())), preferred_element_type=F32
            )
            weight = jnp.exp2(score * SCALE)
            if own is not None:
                r = lax.broadcasted_iota(jnp.int32, (chunk, STEP), 0) + (own + i)
                c = lax.broadcasted_iota(jnp.int32, (chunk, STEP), 1) + j
                weight = jnp.where(r == c, 0.0, weight)
            same = jnp.where(labels == right_labels[:, j : j + STEP], weight, 0.0)
            if rows:
                for k in range(0, STEP, LANES):
                    a, b = weight[:, k : k + LANES], same[:, k : k + LANES]
                    row_total = a if row_total is None else row_total + a
                    row_same = b if row_same is None else row_same + b
            if columns:
                totals.append(jnp.sum(weight, axis=0, keepdims=True))
                sames.append(jnp.sum(same, axis=0, keepdims=True))
        if rows:
            row_parts.append((row_total, row_same))
        if columns:
            both = jnp.concatenate([jnp.concatenate(totals, axis=1), jnp.concatenate(sames, axis=1)], axis=0)
            column = both if column is None else column + both
    rows_out = tuple(jnp.concatenate(p, axis=0) for p in zip(*row_parts)) if rows else None
    return rows_out, column


def add(*pairs):
    total, same = pairs[0]
    for more_total, more_same in pairs[1:]:
        total, same = total + more_total, same + more_same
    return jnp.concatenate([along_lanes(total), along_lanes(same)], axis=0)


def early_part(ref):
    return images(ref, EARLY, 0, EARLY)


def late_part(ref):
    return images(ref, LATE, 0, LATE, head=0)


def row_of(early_ref, late):
    row = label_row(early_ref, EARLY + LATE)
    return row[:, EARLY:] if late else row[:, :EARLY]


def normalise(x_ref, first, held, sems, write):
    rows, parts = held.shape[0], sems.shape[0]
    part = rows // parts
    copies = [
        pltpu.make_async_copy(
            x_ref.at[pl.ds(first + i * part, part), :], held.at[pl.ds(i * part, part), :], sems.at[i]
        )
        for i in range(parts)
    ]
    for copy in copies:
        copy.start()
    for i in range(parts):
        copies[i].wait()
        for q in range(i * part, (i + 1) * part, 64):
            x = held[q : q + 64, :]
            unit = (x * lax.rsqrt(jnp.sum(x * x, axis=1, keepdims=True) + 1e-06)).astype(BF16)
            for k in range(x.shape[1] // LANES):
                write(k, q, unit[:, k * LANES : (k + 1) * LANES])


def unit_early_kernel(x_ref, labels_hbm, out_ref, held, labels_ref, sems, labels_sem):
    labels_copy = pltpu.make_async_copy(labels_hbm, labels_ref, labels_sem)
    labels_copy.start()

    def write(slab, row, unit):
        out_ref[HEAD + slab * EARLY + row : HEAD + slab * EARLY + row + 64, :] = unit

    normalise(x_ref, 0, held, sems, write)
    labels_copy.wait()
    labels = labels_ref[...]
    low = lax.rem(labels, 256)
    blank = jnp.zeros((HEAD - 2 * labels.shape[0], LANES), F32)
    head = jnp.concatenate([(labels - low).astype(F32), low.astype(F32), blank], axis=0)
    out_ref[0:HEAD, :] = head.astype(BF16)


def unit_late_kernel(x_ref, after_ref, out_ref, held, sems):
    def write(slab, row, unit):
        out_ref[slab * LATE + row : slab * LATE + row + 64, :] = unit

    normalise(x_ref, EARLY, held, sems, write)


def own_kernel(ue_ref, ul_ref, own_ref, copy_ref):
    copy_ref[...] = ul_ref[...]
    unit = jnp.concatenate([early_part(ue_ref), late_part(ul_ref)], axis=0)
    labels = label_row(ue_ref, EARLY + LATE)
    _, own = weigh(unit, label_column(ue_ref, EARLY + LATE), unit, labels, False, True, own=0)
    own_ref[...] = own


def partner_kernel(ue_ref, ul_ref, xe_ref, xl_ref, own_in_ref, own_ref, x_labels_ref):
    unit = jnp.concatenate([early_part(ue_ref), late_part(ul_ref)], axis=0)
    labels, x_labels = label_row(ue_ref, EARLY + LATE), label_column(xe_ref, EARLY + LATE)
    x_labels_ref[...] = x_labels
    _, a = weigh(early_part(xe_ref), x_labels[:EARLY], unit, labels, False, True)
    _, b = weigh(late_part(xl_ref), x_labels[EARLY:], unit, labels, False, True)
    own_ref[...] = own_in_ref[...] + a + b


def is_even():
    return lax.rem(lax.axis_index("blk"), 2) == 0


def pick_kernel(p_ref, n_ref, after_ref, out_ref):
    even = is_even()

    @pl.when(even)
    def _():
        out_ref[...] = n_ref[...]

    @pl.when(jnp.logical_not(even))
    def _():
        out_ref[...] = p_ref[...]


def early_kernel(
    ue_ref, ul_ref, xe_ref, xl_ref, pe_ref, ne_ref, x_labels_ref, own_in_ref,
    own_ref, p_ref, n_ref, p_labels_ref, n_labels_ref,
):
    p_labels_ref[...] = label_column(pe_ref, EARLY + LATE)
    n_labels = label_column(ne_ref, EARLY + LATE)
    n_labels_ref[...] = n_labels
    n, labels = early_part(ne_ref), n_labels[:EARLY]
    n1, own1 = weigh(n, labels, early_part(ue_ref), row_of(ue_ref, False), True, True)
    n2, own2 = weigh(n, labels, late_part(ul_ref), row_of(ue_ref, True), True, True)
    n3, p1 = weigh(n, labels, early_part(pe_ref), row_of(pe_ref, False), True, True)
    own_ref[:, :EARLY] = own_in_ref[:, :EARLY] + own1
    own_ref[:, EARLY:] = own_in_ref[:, EARLY:] + own2
    labels = row_of(ne_ref, False)
    _, n4 = weigh(early_part(xe_ref), x_labels_ref[:EARLY], n, labels, False, True)
    _, n5 = weigh(late_part(xl_ref), x_labels_ref[EARLY:], n, labels, False, True)
    n_ref[...] = n4 + n5 + add(n1, n2, n3)
    p, labels = early_part(pe_ref), row_of(pe_ref, False)
    _, p2 = weigh(early_part(xe_ref), x_labels_ref[:EARLY], p, labels, False, True)
    _, p3 = weigh(late_part(xl_ref), x_labels_ref[EARLY:], p, labels, False, True)
    p_ref[...] = p1 + p2 + p3


def early_f_kernel(fe_ref, pe_ref, ne_ref, p_in_ref, n_in_ref, p_ref, n_ref, f_labels_ref):
    even = is_even()
    right = jnp.where(even, early_part(ne_ref), early_part(pe_ref))
    labels = jnp.where(even, row_of(ne_ref, False), row_of(pe_ref, False))
    f_labels = label_column(fe_ref, EARLY + LATE)
    f_labels_ref[...] = f_labels
    _, more = weigh(early_part(fe_ref), f_labels[:EARLY], right, labels, False, True)
    p_ref[...] = p_in_ref[...] + jnp.where(even, 0.0, more)
    n_ref[...] = n_in_ref[...] + jnp.where(even, more, 0.0)


def late_n_kernel(
    ue_ref, ul_ref, xe_ref, xl_ref, pe_ref, ne_ref, nl_ref, x_labels_ref, n_labels_ref, own_in_ref, p_in_ref,
    own_ref, p_ref, n_ref, part_ref,
):
    n, labels = late_part(nl_ref), n_labels_ref[EARLY:]
    n1, own1 = weigh(n, labels, early_part(ue_ref), row_of(ue_ref, False), True, True)
    n2, own2 = weigh(n, labels, late_part(ul_ref), row_of(ue_ref, True), True, True)
    n3, p1 = weigh(n, labels, early_part(pe_ref), row_of(pe_ref, False), True, True)
    for k in range(2):
        part_ref[k] = n1[k] + n2[k] + n3[k]
    labels = row_of(ne_ref, True)
    _, n4 = weigh(early_part(xe_ref), x_labels_ref[:EARLY], n, labels, False, True)
    _, n5 = weigh(late_part(xl_ref), x_labels_ref[EARLY:], n, labels, False, True)
    own_ref[:, :EARLY] = own_in_ref[:, :EARLY] + own1
    own_ref[:, EARLY:] = own_in_ref[:, EARLY:] + own2
    p_ref[...] = p_in_ref[...] + p1
    n_ref[...] = n4 + n5


def late_p_kernel(
    xe_ref, xl_ref, pe_ref, ne_ref, pl_ref, nl_ref, x_labels_ref, p_labels_ref, n_labels_ref,
    p_in_ref, n_in_ref, n_late_ref, n_part_ref, p_ref, n_ref,
):
    p, labels = late_part(pl_ref), row_of(pe_ref, True)
    _, p1 = weigh(early_part(xe_ref), x_labels_ref[:EARLY], p, labels, False, True)
    _, p2 = weigh(late_part(xl_ref), x_labels_ref[EARLY:], p, labels, False, True)
    p3, n1 = weigh(p, p_labels_ref[EARLY:], early_part(ne_ref), row_of(ne_ref, False), True, True)
    n2, p4 = weigh(late_part(nl_ref), n_labels_ref[EARLY:], p, labels, True, True)
    p_ref[:, :EARLY] = p_in_ref[...]
    p_ref[:, EARLY:] = p1 + p2 + p4 + add(p3)
    n_ref[:, :EARLY] = n_in_ref[...] + n1
    n_ref[:, EARLY:] = n_late_ref[...] + add((n_part_ref[0], n_part_ref[1]), n2)


def end_kernel(fe_ref, fl_ref, pe_ref, ne_ref, pl_ref, nl_ref, f_labels_ref, p_in_ref, n_in_ref, p_ref, n_ref):
    even = is_even()
    right = jnp.where(even, early_part(ne_ref), early_part(pe_ref))
    late = jnp.where(even, late_part(nl_ref), late_part(pl_ref))
    labels = jnp.where(even, row_of(ne_ref, False), row_of(pe_ref, False))
    late_labels = jnp.where(even, row_of(ne_ref, True), row_of(pe_ref, True))
    f, f_labels = late_part(fl_ref), f_labels_ref[EARLY:]
    _, a = weigh(f, f_labels, right, labels, False, True)
    _, b = weigh(f, f_labels, late, late_labels, False, True)
    _, c = weigh(early_part(fe_ref), f_labels_ref[:EARLY], late, late_labels, False, True)
    more = jnp.concatenate([a, b + c], axis=1)
    p_ref[...] = p_in_ref[...] + jnp.where(even, 0.0, more)
    n_ref[...] = n_in_ref[...] + jnp.where(even, more, 0.0)


def last_kernel(own_ref, a_ref, b_ref, agreement_ref, log_ref):
    sums = own_ref[...] + a_ref[...] + b_ref[...]
    agreement = sums[1:2] / sums[0:1]
    log_weight = jnp.log(sums[0:1]) - 1.0 / TAU
    for k in range(agreement_ref.shape[0]):
        agreement_ref[k : k + 1, :] = agreement[:, k * LANES : (k + 1) * LANES]
        log_ref[k : k + 1, :] = log_weight[:, k * LANES : (k + 1) * LANES]


def on_device(embeddings, labels):
    n, depth = embeddings.shape
    slabs = depth // LANES
    size = lax.axis_size("blk")
    up = [(i, (i + 2) % size) for i in range(size)]
    down = [(i, (i - 2) % size) for i in range(size)]
    swap = [(i, i ^ 1) for i in range(size)]
    send = lambda array, route: lax.ppermute(array, "blk", route)
    struct = jax.ShapeDtypeStruct
    sums, early_sums = struct((2, n), F32), struct((2, EARLY), F32)
    early, late = struct((HEAD + slabs * EARLY, LANES), BF16), struct((slabs * LATE, LANES), BF16)

    hbm = pl.BlockSpec(memory_space=pltpu.HBM)
    labels = pltpu.with_memory_space_constraint(labels.reshape(n // LANES, LANES), pltpu.HBM)
    ue = call(
        unit_early_kernel,
        early,
        (embeddings, labels),
        "unit_early",
        0.1,
        in_specs=[hbm, hbm],
        scratch=[
            pltpu.VMEM((EARLY, depth), F32),
            pltpu.VMEM((n // LANES, LANES), jnp.int32),
            pltpu.SemaphoreType.DMA((8,)),
            pltpu.SemaphoreType.DMA,
        ],
        limit=52,
    )
    ul = call(
        unit_late_kernel,
        late,
        (embeddings, ue),
        "unit_late",
        0.1,
        in_specs=[hbm, pl.BlockSpec(memory_space=pltpu.VMEM)],
        scratch=[pltpu.VMEM((LATE, depth), F32), pltpu.SemaphoreType.DMA((4,))],
        limit=52,
    )
    pe = send(ue, up)
    ne = send(ue, down)
    xe = send(lax.optimization_barrier((ue, ul))[0], swap)
    xl = send(ul, swap)
    own, copy = call(own_kernel, (sums, late), (ue, ul), "own", 1)
    late_p = send(copy, up)
    late_n = send(copy, down)
    column, late_sums, part = struct((n, LANES), F32), struct((2, LATE), F32), struct((2, LATE, LANES), F32)
    own, x_labels = call(partner_kernel, (sums, column), (ue, ul, xe, xl, own), "with_partner", 1)

    fe = send(call(pick_kernel, early, (pe, ne, own), "pick", 0.1), swap)
    own, p, q, p_labels, q_labels = call(
        early_kernel,
        (sums, early_sums, early_sums, column, column),
        (ue, ul, xe, xl, pe, ne, x_labels, own),
        "early",
        2.5,
    )
    p, q, f_labels = call(
        early_f_kernel, (early_sums, early_sums, column), (fe, pe, ne, p, q), "early_f", 0.5
    )
    own, p, q_late, q_part = call(
        late_n_kernel,
        (sums, early_sums, late_sums, part),
        (ue, ul, xe, xl, pe, ne, late_n, x_labels, q_labels, own, p),
        "late_n",
        1,
    )
    fl = send(call(pick_kernel, late, (late_p, late_n, q_late), "pick_late", 0.1), swap)
    p, q = call(
        late_p_kernel,
        (sums, sums),
        (xe, xl, pe, ne, late_p, late_n, x_labels, p_labels, q_labels, p, q, q_late, q_part),
        "late_p",
        0.7,
    )
    p, q = call(end_kernel, (sums, sums), (fe, fl, pe, ne, late_p, late_n, f_labels, p, q), "end", 0.6)
    from_lower = send(q, up)
    from_upper = send(p, down)
    shape = struct((n // LANES, LANES), F32)
    agreement, log_weight = call(last_kernel, (shape, shape), (own, from_lower, from_upper), "last", 0.01)
    return agreement.reshape(n), log_weight.reshape(n)


def solution(mesh):
    return jax.shard_map(
        on_device,
        mesh=mesh,
        in_specs=(P("blk", None), P("blk")),
        out_specs=(P("blk"), P("blk")),
        check_vma=False,
    )
```

```python
import functools
import math

import jax
import jax.numpy as jnp
from jax import lax
from jax.experimental import pallas as pl
from jax.experimental.pallas import tpu as pltpu
from jax.sharding import PartitionSpec as P

TAU = 0.1
SCALE = math.log2(math.e) / TAU
LANES = 128
HEAD = 16
EARLY = 512
LATE = 256
CHUNK = 512
LONG = 8
STEP = 256
F32 = jnp.float32
BF16 = jnp.bfloat16


def call(kernel, out_shape, operands, name, tiles, in_specs=None, scratch=(), limit=28):
    vmem = pl.BlockSpec(memory_space=pltpu.VMEM)
    return pl.pallas_call(
        kernel,
        out_shape=out_shape,
        in_specs=in_specs or [vmem] * len(operands),
        out_specs=jax.tree.map(lambda _: vmem, out_shape),
        scratch_shapes=scratch,
        name=name,
        cost_estimate=pl.CostEstimate(
            flops=int(1.2e10 * tiles),
            bytes_accessed=1024,
            transcendentals=0,
        ),
        compiler_params=pltpu.CompilerParams(vmem_limit_bytes=limit * 1024 * 1024),
    )(*operands)


def images(ref, n, first, count, head=HEAD):
    slabs = (ref.shape[0] - head) // n
    return jnp.concatenate(
        [ref[head + k * n + first : head + k * n + first + count, :] for k in range(slabs)], axis=1
    )


def label_row(ref, n):
    head = ref[0:HEAD, :].astype(F32)
    groups = n // LANES
    return jnp.concatenate([head[k : k + 1] + head[k + groups : k + groups + 1] for k in range(groups)], axis=1)


def label_column(ref, n):
    groups = n // LANES
    row = lax.broadcasted_iota(jnp.int32, (HEAD, n), 0)
    group = lax.broadcasted_iota(jnp.int32, (HEAD, n), 1) // LANES
    pick = jnp.where((row == group) | (row == group + groups), 1.0, 0.0).astype(BF16)
    spread = lax.dot_general(ref[0:HEAD, :], pick, (((0,), (0,)), ((), ())), preferred_element_type=F32)
    return jnp.concatenate([spread[:, k * LANES : (k + 1) * LANES] for k in range(groups)], axis=0)


def along_lanes(partial):
    return jnp.concatenate(
        [
            jnp.sum(partial[i : i + LANES].T, axis=0, keepdims=True)
            for i in range(0, partial.shape[0], LANES)
        ],
        axis=1,
    )


def weigh(left, left_labels, right, right_labels, rows, columns, own=None):
    m, n = left.shape[0], right.shape[0]
    row_parts, column = [], None
    for i in range(0, m, CHUNK):
        chunk = min(CHUNK, m - i)
        here = left[i : i + chunk]
        labels = jnp.concatenate([left_labels[i : i + chunk]] * (STEP // LANES), axis=1)
        totals, sames, row_total, row_same = [], [], None, None
        for j in range(0, n, STEP):
            score = lax.dot_general(
                here, right[j : j + STEP], (((1,), (1,)), ((), ())), preferred_element_type=F32
            )
            weight = jnp.exp2(score * SCALE)
            if own is not None:
                r = lax.broadcasted_iota(jnp.int32, (chunk, STEP), 0) + (own + i)
                c = lax.broadcasted_iota(jnp.int32, (chunk, STEP), 1) + j
                weight = jnp.where(r == c, 0.0, weight)
            same = jnp.where(labels == right_labels[:, j : j + STEP], weight, 0.0)
            if rows:
                for k in range(0, STEP, LANES):
                    a, b = weight[:, k : k + LANES], same[:, k : k + LANES]
                    row_total = a if row_total is None else row_total + a
                    row_same = b if row_same is None else row_same + b
            if columns:
                totals.append(jnp.sum(weight, axis=0, keepdims=True))
                sames.append(jnp.sum(same, axis=0, keepdims=True))
        if rows:
            row_parts.append((row_total, row_same))
        if columns:
            both = jnp.concatenate([jnp.concatenate(totals, axis=1), jnp.concatenate(sames, axis=1)], axis=0)
            column = both if column is None else column + both
    rows_out = tuple(jnp.concatenate(p, axis=0) for p in zip(*row_parts)) if rows else None
    return rows_out, column


def add(*pairs):
    total, same = pairs[0]
    for more_total, more_same in pairs[1:]:
        total, same = total + more_total, same + more_same
    return jnp.concatenate([along_lanes(total), along_lanes(same)], axis=0)


def early_part(ref):
    return images(ref, EARLY, 0, EARLY)


def late_part(ref):
    return images(ref, LATE, 0, LATE, head=0)


def row_of(early_ref, late):
    row = label_row(early_ref, EARLY + LATE)
    return row[:, EARLY:] if late else row[:, :EARLY]


def normalise(x_ref, first, held, sems, write):
    rows, parts = held.shape[0], sems.shape[0]
    part = rows // parts
    copies = [
        pltpu.make_async_copy(
            x_ref.at[pl.ds(first + i * part, part), :], held.at[pl.ds(i * part, part), :], sems.at[i]
        )
        for i in range(parts)
    ]
    for copy in copies:
        copy.start()
    for i in range(parts):
        copies[i].wait()
        x = held[i * part : (i + 1) * part, :]
        unit = (x * lax.rsqrt(jnp.sum(x * x, axis=1, keepdims=True) + 1e-06)).astype(BF16)
        for k in range(x.shape[1] // LANES):
            write(k, i * part, unit[:, k * LANES : (k + 1) * LANES])


def unit_early_kernel(x_ref, labels_hbm, out_ref, held, labels_ref, sems, labels_sem):
    labels_copy = pltpu.make_async_copy(labels_hbm, labels_ref, labels_sem)
    labels_copy.start()

    def write(slab, row, unit):
        out_ref[HEAD + slab * EARLY + row : HEAD + slab * EARLY + row + unit.shape[0], :] = unit

    normalise(x_ref, 0, held, sems, write)
    labels_copy.wait()
    labels = labels_ref[...]
    low = lax.rem(labels, 256)
    blank = jnp.zeros((HEAD - 2 * labels.shape[0], LANES), F32)
    head = jnp.concatenate([(labels - low).astype(F32), low.astype(F32), blank], axis=0)
    out_ref[0:HEAD, :] = head.astype(BF16)


def unit_late_kernel(x_ref, after_ref, out_ref, held, sems):
    def write(slab, row, unit):
        out_ref[slab * LATE + row : slab * LATE + row + unit.shape[0], :] = unit

    normalise(x_ref, EARLY, held, sems, write)


def own_kernel(ue_ref, ul_ref, own_ref):
    unit = jnp.concatenate([early_part(ue_ref), late_part(ul_ref)], axis=0)
    labels = label_row(ue_ref, EARLY + LATE)
    _, own = weigh(unit, label_column(ue_ref, EARLY + LATE), unit, labels, False, True, own=0)
    own_ref[...] = own


def partner_kernel(ue_ref, ul_ref, xe_ref, xl_ref, own_in_ref, own_ref, x_labels_ref, copy_ref):
    copy_ref[...] = ul_ref[...]
    unit = jnp.concatenate([early_part(ue_ref), late_part(ul_ref)], axis=0)
    labels, x_labels = label_row(ue_ref, EARLY + LATE), label_column(xe_ref, EARLY + LATE)
    x_labels_ref[...] = x_labels
    _, a = weigh(early_part(xe_ref), x_labels[:EARLY], unit, labels, False, True)
    _, b = weigh(late_part(xl_ref), x_labels[EARLY:], unit, labels, False, True)
    own_ref[...] = own_in_ref[...] + a + b


def is_even():
    return lax.rem(lax.axis_index("blk"), 2) == 0


def is_lower():
    return lax.rem(lax.axis_index("blk"), LONG) < 2


def is_upper():
    return lax.rem(lax.axis_index("blk"), LONG) >= LONG - 2


def copy_when(condition, source_ref, out_ref):
    @pl.when(condition)
    def _():
        out_ref[...] = source_ref[...]


def pick_early_kernel(p_ref, n_ref, after_ref, out_ref):
    even = is_even()
    copy_when(even, n_ref, out_ref)
    copy_when(jnp.logical_not(even), p_ref, out_ref)


def pick_late_kernel(p_ref, n_ref, w_ref, after_ref, out_ref):
    even = is_even()
    odd = jnp.logical_not(even)
    copy_when(even & is_upper(), w_ref, out_ref)
    copy_when(even & jnp.logical_not(is_upper()), n_ref, out_ref)
    copy_when(odd & is_lower(), w_ref, out_ref)
    copy_when(odd & jnp.logical_not(is_lower()), p_ref, out_ref)


def labels_kernel(p_ref, after_ref, labels_ref):
    labels_ref[...] = label_column(p_ref, EARLY + LATE)


def early_kernel(
    ue_ref, ul_ref, xe_ref, xl_ref, pe_ref, ne_ref, x_labels_ref, own_in_ref,
    own_ref, p_ref, n_ref, n_labels_ref,
):
    n_labels = label_column(ne_ref, EARLY + LATE)
    n_labels_ref[...] = n_labels
    n, labels = early_part(ne_ref), n_labels[:EARLY]
    n1, own1 = weigh(n, labels, early_part(ue_ref), row_of(ue_ref, False), True, True)
    n2, own2 = weigh(n, labels, late_part(ul_ref), row_of(ue_ref, True), True, True)
    n3, p1 = weigh(n, labels, early_part(pe_ref), row_of(pe_ref, False), True, True)
    own_ref[:, :EARLY] = own_in_ref[:, :EARLY] + own1
    own_ref[:, EARLY:] = own_in_ref[:, EARLY:] + own2
    labels = row_of(ne_ref, False)
    _, n4 = weigh(early_part(xe_ref), x_labels_ref[:EARLY], n, labels, False, True)
    _, n5 = weigh(late_part(xl_ref), x_labels_ref[EARLY:], n, labels, False, True)
    n_ref[...] = n4 + n5 + add(n1, n2, n3)
    p, labels = early_part(pe_ref), row_of(pe_ref, False)
    _, p2 = weigh(early_part(xe_ref), x_labels_ref[:EARLY], p, labels, False, True)
    _, p3 = weigh(late_part(xl_ref), x_labels_ref[EARLY:], p, labels, False, True)
    p_ref[...] = p1 + p2 + p3


def early_f_kernel(fe_ref, re_ref, p_in_ref, n_in_ref, p_ref, n_ref, f_labels_ref):
    even = is_even()
    f_labels = label_column(fe_ref, EARLY + LATE)
    f_labels_ref[...] = f_labels
    _, more = weigh(early_part(fe_ref), f_labels[:EARLY], early_part(re_ref), row_of(re_ref, False), False, True)
    p_ref[...] = p_in_ref[...] + jnp.where(even, 0.0, more)
    n_ref[...] = n_in_ref[...] + jnp.where(even, more, 0.0)


def add_late_n(n_ref, ue_ref, ul_ref, xe_ref, xl_ref, pe_ref, ne_ref, x_labels_ref, n_labels_ref, out):
    own_ref, p_ref, late_ref, part_ref = out
    n, labels = late_part(n_ref), n_labels_ref[EARLY:]
    n1, own1 = weigh(n, labels, early_part(ue_ref), row_of(ue_ref, False), True, True)
    n2, own2 = weigh(n, labels, late_part(ul_ref), row_of(ue_ref, True), True, True)
    n3, p1 = weigh(n, labels, early_part(pe_ref), row_of(pe_ref, False), True, True)
    for k in range(2):
        part_ref[k] = n1[k] + n2[k] + n3[k]
    labels = row_of(ne_ref, True)
    _, n4 = weigh(early_part(xe_ref), x_labels_ref[:EARLY], n, labels, False, True)
    _, n5 = weigh(late_part(xl_ref), x_labels_ref[EARLY:], n, labels, False, True)
    own_ref[:, :EARLY] = own_ref[:, :EARLY] + own1
    own_ref[:, EARLY:] = own_ref[:, EARLY:] + own2
    p_ref[...] = p_ref[...] + p1
    late_ref[...] = n4 + n5


def add_late_p(p_ref, xe_ref, xl_ref, pe_ref, ne_ref, x_labels_ref, p_labels_ref, out):
    n_ref, late_ref = out
    p, labels = late_part(p_ref), row_of(pe_ref, True)
    _, p1 = weigh(early_part(xe_ref), x_labels_ref[:EARLY], p, labels, False, True)
    _, p2 = weigh(late_part(xl_ref), x_labels_ref[EARLY:], p, labels, False, True)
    p3, n1 = weigh(p, p_labels_ref[EARLY:], early_part(ne_ref), row_of(ne_ref, False), True, True)
    n_ref[...] = n_ref[...] + n1
    late_ref[...] = p1 + p2 + add(p3)


def near_kernel(
    pl_ref, nl_ref, ue_ref, ul_ref, xe_ref, xl_ref, ne_ref, pe_ref, x_labels_ref, p_labels_ref, n_labels_ref,
    own_in_ref, p_in_ref, n_in_ref, own_ref, p_ref, n_ref, p_late_ref, n_late_ref, part_ref,
):
    own_ref[...] = own_in_ref[...]
    p_ref[...] = p_in_ref[...]
    n_ref[...] = n_in_ref[...]

    @pl.when(jnp.logical_not(is_upper()))
    def _():
        add_late_n(
            nl_ref, ue_ref, ul_ref, xe_ref, xl_ref, pe_ref, ne_ref, x_labels_ref, n_labels_ref,
            (own_ref, p_ref, n_late_ref, part_ref),
        )

    @pl.when(jnp.logical_not(is_lower()))
    def _():
        add_late_p(pl_ref, xe_ref, xl_ref, pe_ref, ne_ref, x_labels_ref, p_labels_ref, (n_ref, p_late_ref))


def far_kernel(
    w_ref, nl_ref, pl_ref, ue_ref, ul_ref, xe_ref, xl_ref, ne_ref, pe_ref, x_labels_ref, p_labels_ref,
    n_labels_ref, own_in_ref, p_in_ref, n_in_ref, p_late_in_ref, n_late_in_ref, part_in_ref,
    own_ref, p_ref, n_ref, p_early, n_early, p_late, n_late, part,
):
    lower, upper = is_lower(), is_upper()
    own_ref[...] = own_in_ref[...]
    p_early[...] = p_in_ref[...]
    n_early[...] = n_in_ref[...]

    @pl.when(upper)
    def _():
        add_late_n(
            w_ref, ue_ref, ul_ref, xe_ref, xl_ref, pe_ref, ne_ref, x_labels_ref, n_labels_ref,
            (own_ref, p_early, n_late, part),
        )

    @pl.when(jnp.logical_not(upper))
    def _():
        n_late[...] = n_late_in_ref[...]
        part[...] = part_in_ref[...]

    @pl.when(lower)
    def _():
        add_late_p(w_ref, xe_ref, xl_ref, pe_ref, ne_ref, x_labels_ref, p_labels_ref, (n_early, p_late))

    copy_when(jnp.logical_not(lower), p_late_in_ref, p_late)
    w = late_part(w_ref)
    n = jnp.where(upper, w, late_part(nl_ref))
    p = jnp.where(lower, w, late_part(pl_ref))
    n1, p1 = weigh(n, n_labels_ref[EARLY:], p, row_of(pe_ref, True), True, True)
    p_ref[:, :EARLY] = p_early[...]
    p_ref[:, EARLY:] = p_late[...] + p1
    n_ref[:, :EARLY] = n_early[...]
    n_ref[:, EARLY:] = n_late[...] + add((part[0], part[1]), n1)


def end_kernel(fe_ref, fl_ref, re_ref, rl_ref, f_labels_ref, p_in_ref, n_in_ref, p_ref, n_ref):
    even = is_even()
    labels, late_labels = row_of(re_ref, False), row_of(re_ref, True)
    late = late_part(rl_ref)
    f, f_labels = late_part(fl_ref), f_labels_ref[EARLY:]
    _, a = weigh(f, f_labels, early_part(re_ref), labels, False, True)
    _, b = weigh(f, f_labels, late, late_labels, False, True)
    _, c = weigh(early_part(fe_ref), f_labels_ref[:EARLY], late, late_labels, False, True)
    more = jnp.concatenate([a, b + c], axis=1)
    p_ref[...] = p_in_ref[...] + jnp.where(even, 0.0, more)
    n_ref[...] = n_in_ref[...] + jnp.where(even, more, 0.0)


def last_kernel(own_ref, a_ref, b_ref, agreement_ref, log_ref):
    sums = own_ref[...] + a_ref[...] + b_ref[...]
    agreement = sums[1:2] / sums[0:1]
    log_weight = jnp.log(sums[0:1]) - 1.0 / TAU
    for k in range(agreement_ref.shape[0]):
        agreement_ref[k : k + 1, :] = agreement[:, k * LANES : (k + 1) * LANES]
        log_ref[k : k + 1, :] = log_weight[:, k * LANES : (k + 1) * LANES]


def on_device(embeddings, labels):
    n, depth = embeddings.shape
    slabs = depth // LANES
    size = lax.axis_size("blk")
    up = [(i, (i + 2) % size) for i in range(size)]
    down = [(i, (i - 2) % size) for i in range(size)]
    swap = [(i, i ^ 1) for i in range(size)]
    send = lambda array, route: lax.ppermute(array, "blk", route)
    struct = jax.ShapeDtypeStruct
    sums, early_sums = struct((2, n), F32), struct((2, EARLY), F32)
    early, late = struct((HEAD + slabs * EARLY, LANES), BF16), struct((slabs * LATE, LANES), BF16)

    hbm = pl.BlockSpec(memory_space=pltpu.HBM)
    labels = pltpu.with_memory_space_constraint(labels.reshape(n // LANES, LANES), pltpu.HBM)
    ue = call(
        unit_early_kernel,
        early,
        (embeddings, labels),
        "unit_early",
        0.1,
        in_specs=[hbm, hbm],
        scratch=[
            pltpu.VMEM((EARLY, depth), F32),
            pltpu.VMEM((n // LANES, LANES), jnp.int32),
            pltpu.SemaphoreType.DMA((4,)),
            pltpu.SemaphoreType.DMA,
        ],
        limit=52,
    )
    ul = call(
        unit_late_kernel,
        late,
        (embeddings, ue),
        "unit_late",
        0.1,
        in_specs=[hbm, pl.BlockSpec(memory_space=pltpu.VMEM)],
        scratch=[pltpu.VMEM((LATE, depth), F32), pltpu.SemaphoreType.DMA((2,))],
        limit=52,
    )
    pe = send(ue, up)
    ne = send(ue, down)
    xe = send(lax.optimization_barrier((ue, ul))[0], swap)
    xl = send(ul, swap)
    own = call(own_kernel, sums, (ue, ul), "own", 1)
    column, late_sums, part = struct((n, LANES), F32), struct((2, LATE), F32), struct((2, LATE, LANES), F32)
    own, x_labels, copy = call(partner_kernel, (sums, column, late), (ue, ul, xe, xl, own), "with_partner", 1)
    upper = [i for i in range(size) if i % LONG >= LONG - 2]
    far = [(i, (i + 2) % size) for i in upper] + [((i + 2) % size, i) for i in upper]
    late_p = send(copy, [pair for pair in up if pair not in far])
    late_n = send(copy, [pair for pair in down if pair not in far])
    late_w = send(copy, far)

    p_labels = call(labels_kernel, column, (pe, own), "labels", 0.1)
    re = call(pick_early_kernel, early, (pe, ne, p_labels), "pick", 0.1)
    fe = send(re, swap)
    own, p, q, q_labels = call(
        early_kernel,
        (sums, early_sums, early_sums, column),
        (ue, ul, xe, xl, pe, ne, x_labels, own),
        "early",
        2.5,
    )
    p, q, f_labels = call(early_f_kernel, (early_sums, early_sums, column), (fe, re, p, q), "early_f", 0.5)
    fixed = (ue, ul, xe, xl, ne, pe, x_labels, p_labels, q_labels)
    own, p, q, p_late, q_late, q_part = call(
        near_kernel,
        (sums, early_sums, early_sums, late_sums, late_sums, part),
        (late_p, late_n, *fixed, own, p, q),
        "near",
        1.7,
    )
    rl = call(pick_late_kernel, late, (late_p, late_n, late_w, q), "pick_late", 0.1)
    fl = send(rl, swap)
    vmem = lambda shape: pltpu.VMEM(shape.shape, shape.dtype)
    own, p, q = call(
        far_kernel,
        (sums, sums, sums),
        (late_w, late_n, late_p, *fixed, own, p, q, p_late, q_late, q_part),
        "far",
        0.2,
        scratch=[vmem(early_sums), vmem(early_sums), vmem(late_sums), vmem(late_sums), vmem(part)],
    )
    p, q = call(end_kernel, (sums, sums), (fe, fl, re, rl, f_labels, p, q), "end", 0.6)
    from_lower = send(q, up)
    from_upper = send(p, down)
    shape = struct((n // LANES, LANES), F32)
    agreement, log_weight = call(last_kernel, (shape, shape), (own, from_lower, from_upper), "last", 0.01)
    return agreement.reshape(n), log_weight.reshape(n)


def solution(mesh):
    return jax.shard_map(
        on_device,
        mesh=mesh,
        in_specs=(P("blk", None), P("blk")),
        out_specs=(P("blk"), P("blk")),
        check_vma=False,
    )
```

```python
import functools
import math

import jax
import jax.numpy as jnp
from jax import lax
from jax.experimental import pallas as pl
from jax.experimental.pallas import tpu as pltpu
from jax.sharding import PartitionSpec as P

TAU = 0.1
SCALE = math.log2(math.e) / TAU
LANES = 128
HEAD = 16
EARLY = 512
LATE = 256
CHUNK = 512
LONG = 8
STEP = 256
F32 = jnp.float32
BF16 = jnp.bfloat16


def call(kernel, out_shape, operands, name, tiles, in_specs=None, scratch=(), limit=28):
    vmem = pl.BlockSpec(memory_space=pltpu.VMEM)
    return pl.pallas_call(
        kernel,
        out_shape=out_shape,
        in_specs=in_specs or [vmem] * len(operands),
        out_specs=jax.tree.map(lambda _: vmem, out_shape),
        scratch_shapes=scratch,
        name=name,
        cost_estimate=pl.CostEstimate(
            flops=int(1.2e10 * tiles),
            bytes_accessed=1024,
            transcendentals=0,
        ),
        compiler_params=pltpu.CompilerParams(vmem_limit_bytes=limit * 1024 * 1024),
    )(*operands)


def images(ref, n, first, count, head=HEAD):
    slabs = (ref.shape[0] - head) // n
    return jnp.concatenate(
        [ref[head + k * n + first : head + k * n + first + count, :] for k in range(slabs)], axis=1
    )


def label_row(ref, n):
    head = ref[0:HEAD, :].astype(F32)
    groups = n // LANES
    return jnp.concatenate([head[k : k + 1] + head[k + groups : k + groups + 1] for k in range(groups)], axis=1)


def label_column(ref, n):
    groups = n // LANES
    row = lax.broadcasted_iota(jnp.int32, (HEAD, n), 0)
    group = lax.broadcasted_iota(jnp.int32, (HEAD, n), 1) // LANES
    pick = jnp.where((row == group) | (row == group + groups), 1.0, 0.0).astype(BF16)
    spread = lax.dot_general(ref[0:HEAD, :], pick, (((0,), (0,)), ((), ())), preferred_element_type=F32)
    return jnp.concatenate([spread[:, k * LANES : (k + 1) * LANES] for k in range(groups)], axis=0)


def along_lanes(partial):
    return jnp.concatenate(
        [
            jnp.sum(partial[i : i + LANES].T, axis=0, keepdims=True)
            for i in range(0, partial.shape[0], LANES)
        ],
        axis=1,
    )


def weigh(left, left_labels, right, right_labels, rows, columns, own=None):
    m, n = left.shape[0], right.shape[0]
    row_parts, column = [], None
    for i in range(0, m, CHUNK):
        chunk = min(CHUNK, m - i)
        here = left[i : i + chunk]
        labels = jnp.concatenate([left_labels[i : i + chunk]] * (STEP // LANES), axis=1)
        totals, sames, row_total, row_same = [], [], None, None
        for j in range(0, n, STEP):
            score = lax.dot_general(
                here, right[j : j + STEP], (((1,), (1,)), ((), ())), preferred_element_type=F32
            )
            weight = jnp.exp2(score * SCALE)
            if own is not None:
                r = lax.broadcasted_iota(jnp.int32, (chunk, STEP), 0) + (own + i)
                c = lax.broadcasted_iota(jnp.int32, (chunk, STEP), 1) + j
                weight = jnp.where(r == c, 0.0, weight)
            same = jnp.where(labels == right_labels[:, j : j + STEP], weight, 0.0)
            if rows:
                for k in range(0, STEP, LANES):
                    a, b = weight[:, k : k + LANES], same[:, k : k + LANES]
                    row_total = a if row_total is None else row_total + a
                    row_same = b if row_same is None else row_same + b
            if columns:
                totals.append(jnp.sum(weight, axis=0, keepdims=True))
                sames.append(jnp.sum(same, axis=0, keepdims=True))
        if rows:
            row_parts.append((row_total, row_same))
        if columns:
            both = jnp.concatenate([jnp.concatenate(totals, axis=1), jnp.concatenate(sames, axis=1)], axis=0)
            column = both if column is None else column + both
    rows_out = tuple(jnp.concatenate(p, axis=0) for p in zip(*row_parts)) if rows else None
    return rows_out, column


def add(*pairs):
    total, same = pairs[0]
    for more_total, more_same in pairs[1:]:
        total, same = total + more_total, same + more_same
    return jnp.concatenate([along_lanes(total), along_lanes(same)], axis=0)


def early_part(ref):
    return images(ref, EARLY, 0, EARLY)


def late_part(ref):
    return images(ref, LATE, 0, LATE, head=0)


def row_of(early_ref, late):
    row = label_row(early_ref, EARLY + LATE)
    return row[:, EARLY:] if late else row[:, :EARLY]


def normalise(x_ref, first, held, sems, write):
    rows, parts = held.shape[0], sems.shape[0]
    part = rows // parts
    copies = [
        pltpu.make_async_copy(
            x_ref.at[pl.ds(first + i * part, part), :], held.at[pl.ds(i * part, part), :], sems.at[i]
        )
        for i in range(parts)
    ]
    for copy in copies:
        copy.start()
    for i in range(parts):
        copies[i].wait()
        x = held[i * part : (i + 1) * part, :]
        unit = (x * lax.rsqrt(jnp.sum(x * x, axis=1, keepdims=True) + 1e-06)).astype(BF16)
        for k in range(x.shape[1] // LANES):
            write(k, i * part, unit[:, k * LANES : (k + 1) * LANES])


def unit_early_kernel(x_ref, labels_hbm, out_ref, held, labels_ref, sems, labels_sem):
    labels_copy = pltpu.make_async_copy(labels_hbm, labels_ref, labels_sem)
    labels_copy.start()

    def write(slab, row, unit):
        out_ref[HEAD + slab * EARLY + row : HEAD + slab * EARLY + row + unit.shape[0], :] = unit

    normalise(x_ref, 0, held, sems, write)
    labels_copy.wait()
    labels = labels_ref[...]
    low = lax.rem(labels, 256)
    blank = jnp.zeros((HEAD - 2 * labels.shape[0], LANES), F32)
    head = jnp.concatenate([(labels - low).astype(F32), low.astype(F32), blank], axis=0)
    out_ref[0:HEAD, :] = head.astype(BF16)


def unit_late_kernel(x_ref, after_ref, out_ref, held, sems):
    def write(slab, row, unit):
        out_ref[slab * LATE + row : slab * LATE + row + unit.shape[0], :] = unit

    normalise(x_ref, EARLY, held, sems, write)


def own_kernel(ue_ref, ul_ref, own_ref):
    unit = jnp.concatenate([early_part(ue_ref), late_part(ul_ref)], axis=0)
    labels = label_row(ue_ref, EARLY + LATE)
    _, own = weigh(unit, label_column(ue_ref, EARLY + LATE), unit, labels, False, True, own=0)
    own_ref[...] = own


def partner_kernel(ue_ref, ul_ref, xe_ref, xl_ref, own_in_ref, own_ref, x_labels_ref, copy_ref):
    copy_ref[...] = ul_ref[...]
    unit = jnp.concatenate([early_part(ue_ref), late_part(ul_ref)], axis=0)
    labels, x_labels = label_row(ue_ref, EARLY + LATE), label_column(xe_ref, EARLY + LATE)
    x_labels_ref[...] = x_labels
    _, a = weigh(early_part(xe_ref), x_labels[:EARLY], unit, labels, False, True)
    _, b = weigh(late_part(xl_ref), x_labels[EARLY:], unit, labels, False, True)
    own_ref[...] = own_in_ref[...] + a + b


def is_even():
    return lax.rem(lax.axis_index("blk"), 2) == 0


def is_lower():
    return lax.rem(lax.axis_index("blk"), LONG) < 2


def is_upper():
    return lax.rem(lax.axis_index("blk"), LONG) >= LONG - 2


def copy_when(condition, source_ref, out_ref):
    @pl.when(condition)
    def _():
        out_ref[...] = source_ref[...]


def pick_early_kernel(p_ref, n_ref, after_ref, out_ref):
    even = is_even()
    copy_when(even, n_ref, out_ref)
    copy_when(jnp.logical_not(even), p_ref, out_ref)


def pick_late_kernel(p_ref, n_ref, w_ref, after_ref, out_ref):
    even = is_even()
    odd = jnp.logical_not(even)
    copy_when(even & is_upper(), w_ref, out_ref)
    copy_when(even & jnp.logical_not(is_upper()), n_ref, out_ref)
    copy_when(odd & is_lower(), w_ref, out_ref)
    copy_when(odd & jnp.logical_not(is_lower()), p_ref, out_ref)


def labels_kernel(p_ref, after_ref, labels_ref):
    labels_ref[...] = label_column(p_ref, EARLY + LATE)


def early_kernel(
    ue_ref, ul_ref, xe_ref, xl_ref, pe_ref, ne_ref, x_labels_ref, own_in_ref,
    own_ref, p_ref, n_ref, n_labels_ref,
):
    n_labels = label_column(ne_ref, EARLY + LATE)
    n_labels_ref[...] = n_labels
    n, labels = early_part(ne_ref), n_labels[:EARLY]
    n1, own1 = weigh(n, labels, early_part(ue_ref), row_of(ue_ref, False), True, True)
    n2, own2 = weigh(n, labels, late_part(ul_ref), row_of(ue_ref, True), True, True)
    n3, p1 = weigh(n, labels, early_part(pe_ref), row_of(pe_ref, False), True, True)
    own_ref[:, :EARLY] = own_in_ref[:, :EARLY] + own1
    own_ref[:, EARLY:] = own_in_ref[:, EARLY:] + own2
    labels = row_of(ne_ref, False)
    _, n4 = weigh(early_part(xe_ref), x_labels_ref[:EARLY], n, labels, False, True)
    _, n5 = weigh(late_part(xl_ref), x_labels_ref[EARLY:], n, labels, False, True)
    n_ref[...] = n4 + n5 + add(n1, n2, n3)
    p, labels = early_part(pe_ref), row_of(pe_ref, False)
    _, p2 = weigh(early_part(xe_ref), x_labels_ref[:EARLY], p, labels, False, True)
    _, p3 = weigh(late_part(xl_ref), x_labels_ref[EARLY:], p, labels, False, True)
    p_ref[...] = p1 + p2 + p3


def early_f_kernel(fe_ref, re_ref, p_in_ref, n_in_ref, p_ref, n_ref, f_labels_ref):
    even = is_even()
    f_labels = label_column(fe_ref, EARLY + LATE)
    f_labels_ref[...] = f_labels
    _, more = weigh(early_part(fe_ref), f_labels[:EARLY], early_part(re_ref), row_of(re_ref, False), False, True)
    p_ref[...] = p_in_ref[...] + jnp.where(even, 0.0, more)
    n_ref[...] = n_in_ref[...] + jnp.where(even, more, 0.0)


def with_late_n(n_ref, ue_ref, ul_ref, xe_ref, xl_ref, pe_ref, ne_ref, n_labels_ref):
    n, labels = late_part(n_ref), n_labels_ref[EARLY:]
    n1, own1 = weigh(n, labels, early_part(ue_ref), row_of(ue_ref, False), True, True)
    n2, own2 = weigh(n, labels, late_part(ul_ref), row_of(ue_ref, True), True, True)
    n3, p1 = weigh(n, labels, early_part(pe_ref), row_of(pe_ref, False), True, True)
    n4, _ = weigh(n, labels, early_part(xe_ref), row_of(xe_ref, False), True, False)
    n5, _ = weigh(n, labels, late_part(xl_ref), row_of(xe_ref, True), True, False)
    return (n1, n2, n3, n4, n5), own1, own2, p1


def with_late_p(p_ref, xe_ref, xl_ref, pe_ref, ne_ref, p_labels_ref):
    p, labels = late_part(p_ref), p_labels_ref[EARLY:]
    p1, n1 = weigh(p, labels, early_part(ne_ref), row_of(ne_ref, False), True, True)
    p2, _ = weigh(p, labels, early_part(xe_ref), row_of(xe_ref, False), True, False)
    p3, _ = weigh(p, labels, late_part(xl_ref), row_of(xe_ref, True), True, False)
    return (p1, p2, p3), n1


def near_kernel(
    pl_ref, nl_ref, ue_ref, ul_ref, xe_ref, xl_ref, ne_ref, pe_ref, p_labels_ref, n_labels_ref,
    own_in_ref, p_in_ref, n_in_ref, own_ref, p_ref, n_ref, p_late_ref, n_late_ref,
):
    upper, lower = is_upper(), is_lower()
    copy_when(upper, own_in_ref, own_ref)
    copy_when(upper, p_in_ref, p_ref)
    copy_when(lower, n_in_ref, n_ref)

    @pl.when(jnp.logical_not(upper))
    def _():
        n, own1, own2, p1 = with_late_n(nl_ref, ue_ref, ul_ref, xe_ref, xl_ref, pe_ref, ne_ref, n_labels_ref)
        own_ref[:, :EARLY] = own_in_ref[:, :EARLY] + own1
        own_ref[:, EARLY:] = own_in_ref[:, EARLY:] + own2
        p_ref[...] = p_in_ref[...] + p1
        n_late_ref[...] = add(*n)

    @pl.when(jnp.logical_not(lower))
    def _():
        p, n1 = with_late_p(pl_ref, xe_ref, xl_ref, pe_ref, ne_ref, p_labels_ref)
        n_ref[...] = n_in_ref[...] + n1
        p_late_ref[...] = add(*p)


def far_kernel(
    w_ref, nl_ref, pl_ref, ue_ref, ul_ref, xe_ref, xl_ref, ne_ref, pe_ref, p_labels_ref, n_labels_ref,
    own_in_ref, p_in_ref, n_in_ref, p_late_ref, n_late_ref, fe_ref, re_ref, rl_ref, f_labels_ref,
    own_ref, p_ref, n_ref,
):
    upper, lower = is_upper(), is_lower()

    @pl.when(upper)
    def _():
        n, own1, own2, p1 = with_late_n(w_ref, ue_ref, ul_ref, xe_ref, xl_ref, pe_ref, ne_ref, n_labels_ref)
        labels = n_labels_ref[EARLY:]
        n6, p2 = weigh(late_part(w_ref), labels, late_part(pl_ref), row_of(pe_ref, True), True, True)
        own_ref[:, :EARLY] = own_in_ref[:, :EARLY] + own1
        own_ref[:, EARLY:] = own_in_ref[:, EARLY:] + own2
        p_ref[:, :EARLY] = p_in_ref[...] + p1
        p_ref[:, EARLY:] = p_late_ref[...] + p2
        n_ref[:, :EARLY] = n_in_ref[...]
        n_ref[:, EARLY:] = add(*n, n6)

    @pl.when(jnp.logical_not(upper))
    def _():
        own_ref[...] = own_in_ref[...]
        p_ref[:, :EARLY] = p_in_ref[...]

    @pl.when(lower)
    def _():
        p, n1 = with_late_p(w_ref, xe_ref, xl_ref, pe_ref, ne_ref, p_labels_ref)
        labels = p_labels_ref[EARLY:]
        p4, n2 = weigh(late_part(w_ref), labels, late_part(nl_ref), row_of(ne_ref, True), True, True)
        p_ref[:, EARLY:] = add(*p, p4)
        n_ref[:, :EARLY] = n_in_ref[...] + n1
        n_ref[:, EARLY:] = n_late_ref[...] + n2

    @pl.when(jnp.logical_not(lower | upper))
    def _():
        labels = p_labels_ref[EARLY:]
        p1, n1 = weigh(late_part(pl_ref), labels, late_part(nl_ref), row_of(ne_ref, True), True, True)
        p_ref[:, EARLY:] = p_late_ref[...] + add(p1)
        n_ref[:, :EARLY] = n_in_ref[...]
        n_ref[:, EARLY:] = n_late_ref[...] + n1

    _, more = weigh(
        early_part(fe_ref), f_labels_ref[:EARLY], late_part(rl_ref), row_of(re_ref, True), False, True
    )
    even = is_even()
    p_ref[:, EARLY:] = p_ref[:, EARLY:] + jnp.where(even, 0.0, more)
    n_ref[:, EARLY:] = n_ref[:, EARLY:] + jnp.where(even, more, 0.0)


def end_kernel(fl_ref, re_ref, rl_ref, f_labels_ref, p_in_ref, n_in_ref, p_ref, n_ref):
    even = is_even()
    f, labels = late_part(fl_ref), f_labels_ref[EARLY:]
    _, a = weigh(f, labels, early_part(re_ref), row_of(re_ref, False), False, True)
    _, b = weigh(f, labels, late_part(rl_ref), row_of(re_ref, True), False, True)
    more = jnp.concatenate([a, b], axis=1)
    p_ref[...] = p_in_ref[...] + jnp.where(even, 0.0, more)
    n_ref[...] = n_in_ref[...] + jnp.where(even, more, 0.0)


def last_kernel(own_ref, a_ref, b_ref, agreement_ref, log_ref):
    sums = own_ref[...] + a_ref[...] + b_ref[...]
    agreement = sums[1:2] / sums[0:1]
    log_weight = jnp.log(sums[0:1] * math.exp(-1.0 / TAU))
    for k in range(agreement_ref.shape[0]):
        agreement_ref[k : k + 1, :] = agreement[:, k * LANES : (k + 1) * LANES]
        log_ref[k : k + 1, :] = log_weight[:, k * LANES : (k + 1) * LANES]


def on_device(embeddings, labels):
    n, depth = embeddings.shape
    slabs = depth // LANES
    size = lax.axis_size("blk")
    up = [(i, (i + 2) % size) for i in range(size)]
    down = [(i, (i - 2) % size) for i in range(size)]
    swap = [(i, i ^ 1) for i in range(size)]
    send = lambda array, route: lax.ppermute(array, "blk", route)
    struct = jax.ShapeDtypeStruct
    sums, early_sums = struct((2, n), F32), struct((2, EARLY), F32)
    early, late = struct((HEAD + slabs * EARLY, LANES), BF16), struct((slabs * LATE, LANES), BF16)

    hbm = pl.BlockSpec(memory_space=pltpu.HBM)
    labels = pltpu.with_memory_space_constraint(labels.reshape(n // LANES, LANES), pltpu.HBM)
    ue = call(
        unit_early_kernel,
        early,
        (embeddings, labels),
        "unit_early",
        0.1,
        in_specs=[hbm, hbm],
        scratch=[
            pltpu.VMEM((EARLY, depth), F32),
            pltpu.VMEM((n // LANES, LANES), jnp.int32),
            pltpu.SemaphoreType.DMA((2,)),
            pltpu.SemaphoreType.DMA,
        ],
        limit=52,
    )
    ul = call(
        unit_late_kernel,
        late,
        (embeddings, ue),
        "unit_late",
        0.1,
        in_specs=[hbm, pl.BlockSpec(memory_space=pltpu.VMEM)],
        scratch=[pltpu.VMEM((LATE, depth), F32), pltpu.SemaphoreType.DMA((2,))],
        limit=52,
    )
    pe = send(ue, up)
    ne = send(ue, down)
    xe = send(lax.optimization_barrier((ue, ul))[0], swap)
    xl = send(ul, swap)
    own = call(own_kernel, sums, (ue, ul), "own", 1)
    column, late_sums = struct((n, LANES), F32), struct((2, LATE), F32)
    own, x_labels, copy = call(partner_kernel, (sums, column, late), (ue, ul, xe, xl, own), "with_partner", 1)
    upper = [i for i in range(size) if i % LONG >= LONG - 2]
    far = [(i, (i + 2) % size) for i in upper] + [((i + 2) % size, i) for i in upper]
    late_p = send(copy, [pair for pair in up if pair not in far])
    late_n = send(copy, [pair for pair in down if pair not in far])
    late_w = send(copy, far)

    p_labels = call(labels_kernel, column, (pe, own), "labels", 0.1)
    re = call(pick_early_kernel, early, (pe, ne, p_labels), "pick", 0.1)
    fe = send(re, swap)
    own, p, q, q_labels = call(
        early_kernel,
        (sums, early_sums, early_sums, column),
        (ue, ul, xe, xl, pe, ne, x_labels, own),
        "early",
        2.5,
    )
    p, q, f_labels = call(early_f_kernel, (early_sums, early_sums, column), (fe, re, p, q), "early_f", 0.5)
    fixed = (ue, ul, xe, xl, ne, pe, p_labels, q_labels)
    own, p, q, p_late, q_late = call(
        near_kernel,
        (sums, early_sums, early_sums, late_sums, late_sums),
        (late_p, late_n, *fixed, own, p, q),
        "near",
        1.7,
    )
    rl = call(pick_late_kernel, late, (late_p, late_n, late_w, q), "pick_late", 0.1)
    fl = send(rl, swap)
    own, p, q = call(
        far_kernel,
        (sums, sums, sums),
        (late_w, late_n, late_p, *fixed, own, p, q, p_late, q_late, fe, re, rl, f_labels),
        "far",
        0.2,
    )
    p, q = call(end_kernel, (sums, sums), (fl, re, rl, f_labels, p, q), "end", 0.6)
    from_lower = send(q, up)
    from_upper = send(p, down)
    shape = struct((n // LANES, LANES), F32)
    agreement, log_weight = call(last_kernel, (shape, shape), (own, from_lower, from_upper), "last", 0.01)
    return agreement.reshape(n), log_weight.reshape(n)


def solution(mesh):
    return jax.shard_map(
        on_device,
        mesh=mesh,
        in_specs=(P("blk", None), P("blk")),
        out_specs=(P("blk"), P("blk")),
        check_vma=False,
    )
```

```python
import functools
import math

import jax
import jax.numpy as jnp
from jax import lax
from jax.experimental import pallas as pl
from jax.experimental.pallas import tpu as pltpu
from jax.sharding import PartitionSpec as P

TAU = 0.1
SCALE = math.log2(math.e) / TAU
LANES = 128
HEAD = 16
EARLY = 512
LATE = 256
CHUNK = 512
LONG = 8
STEP = 256
F32 = jnp.float32
BF16 = jnp.bfloat16


def call(kernel, out_shape, operands, name, tiles, in_specs=None, scratch=(), limit=28):
    vmem = pl.BlockSpec(memory_space=pltpu.VMEM)
    return pl.pallas_call(
        kernel,
        out_shape=out_shape,
        in_specs=in_specs or [vmem] * len(operands),
        out_specs=jax.tree.map(lambda _: vmem, out_shape),
        scratch_shapes=scratch,
        name=name,
        cost_estimate=pl.CostEstimate(
            flops=int(1.2e10 * tiles),
            bytes_accessed=1024,
            transcendentals=0,
        ),
        compiler_params=pltpu.CompilerParams(vmem_limit_bytes=limit * 1024 * 1024),
    )(*operands)


def images(ref, n, first, count, head=HEAD):
    slabs = (ref.shape[0] - head) // n
    return jnp.concatenate(
        [ref[head + k * n + first : head + k * n + first + count, :] for k in range(slabs)], axis=1
    )


def label_row(ref, n):
    head = ref[0:HEAD, :].astype(F32)
    groups = n // LANES
    return jnp.concatenate([head[k : k + 1] + head[k + groups : k + groups + 1] for k in range(groups)], axis=1)


def label_column(ref, n):
    groups = n // LANES
    row = lax.broadcasted_iota(jnp.int32, (HEAD, n), 0)
    group = lax.broadcasted_iota(jnp.int32, (HEAD, n), 1) // LANES
    pick = jnp.where((row == group) | (row == group + groups), 1.0, 0.0).astype(BF16)
    spread = lax.dot_general(ref[0:HEAD, :], pick, (((0,), (0,)), ((), ())), preferred_element_type=F32)
    return jnp.concatenate([spread[:, k * LANES : (k + 1) * LANES] for k in range(groups)], axis=0)


def along_lanes(partial):
    return jnp.concatenate(
        [
            jnp.sum(partial[i : i + LANES].T, axis=0, keepdims=True)
            for i in range(0, partial.shape[0], LANES)
        ],
        axis=1,
    )


def weigh(left, left_labels, right, right_labels, rows, columns, own=None):
    m, n = left.shape[0], right.shape[0]
    row_parts, column = [], None
    for i in range(0, m, CHUNK):
        chunk = min(CHUNK, m - i)
        here = left[i : i + chunk]
        labels = jnp.concatenate([left_labels[i : i + chunk]] * (STEP // LANES), axis=1)
        totals, sames, row_total, row_same = [], [], None, None
        for j in range(0, n, STEP):
            score = lax.dot_general(
                here, right[j : j + STEP], (((1,), (1,)), ((), ())), preferred_element_type=F32
            )
            weight = jnp.exp2(score * SCALE)
            if own is not None:
                r = lax.broadcasted_iota(jnp.int32, (chunk, STEP), 0) + (own + i)
                c = lax.broadcasted_iota(jnp.int32, (chunk, STEP), 1) + j
                weight = jnp.where(r == c, 0.0, weight)
            same = jnp.where(labels == right_labels[:, j : j + STEP], weight, 0.0)
            if rows:
                for k in range(0, STEP, LANES):
                    a, b = weight[:, k : k + LANES], same[:, k : k + LANES]
                    row_total = a if row_total is None else row_total + a
                    row_same = b if row_same is None else row_same + b
            if columns:
                totals.append(jnp.sum(weight, axis=0, keepdims=True))
                sames.append(jnp.sum(same, axis=0, keepdims=True))
        if rows:
            row_parts.append((row_total, row_same))
        if columns:
            both = jnp.concatenate([jnp.concatenate(totals, axis=1), jnp.concatenate(sames, axis=1)], axis=0)
            column = both if column is None else column + both
    rows_out = tuple(jnp.concatenate(p, axis=0) for p in zip(*row_parts)) if rows else None
    return rows_out, column


def add(*pairs):
    total, same = pairs[0]
    for more_total, more_same in pairs[1:]:
        total, same = total + more_total, same + more_same
    return jnp.concatenate([along_lanes(total), along_lanes(same)], axis=0)


def early_part(ref):
    return images(ref, EARLY, 0, EARLY)


def late_part(ref):
    return images(ref, LATE, 0, LATE, head=0)


def row_of(early_ref, late):
    row = label_row(early_ref, EARLY + LATE)
    return row[:, EARLY:] if late else row[:, :EARLY]


def normalise(x_ref, first, held, sems, write):
    rows, parts = held.shape[0], sems.shape[0]
    part = rows // parts
    copies = [
        pltpu.make_async_copy(
            x_ref.at[pl.ds(first + i * part, part), :], held.at[pl.ds(i * part, part), :], sems.at[i]
        )
        for i in range(parts)
    ]
    for copy in copies:
        copy.start()
    for i in range(parts):
        copies[i].wait()
        x = held[i * part : (i + 1) * part, :]
        unit = (x * lax.rsqrt(jnp.sum(x * x, axis=1, keepdims=True) + 1e-06)).astype(BF16)
        for k in range(x.shape[1] // LANES):
            write(k, i * part, unit[:, k * LANES : (k + 1) * LANES])


def unit_early_kernel(x_ref, labels_hbm, out_ref, held, labels_ref, sems, labels_sem):
    labels_copy = pltpu.make_async_copy(labels_hbm, labels_ref, labels_sem)
    labels_copy.start()

    def write(slab, row, unit):
        out_ref[HEAD + slab * EARLY + row : HEAD + slab * EARLY + row + unit.shape[0], :] = unit

    normalise(x_ref, 0, held, sems, write)
    labels_copy.wait()
    labels = labels_ref[...]
    low = lax.rem(labels, 256)
    blank = jnp.zeros((HEAD - 2 * labels.shape[0], LANES), F32)
    head = jnp.concatenate([(labels - low).astype(F32), low.astype(F32), blank], axis=0)
    out_ref[0:HEAD, :] = head.astype(BF16)


def unit_late_kernel(x_ref, after_ref, out_ref, held, sems):
    def write(slab, row, unit):
        out_ref[slab * LATE + row : slab * LATE + row + unit.shape[0], :] = unit

    normalise(x_ref, EARLY, held, sems, write)


def own_kernel(ue_ref, ul_ref, own_ref):
    unit = jnp.concatenate([early_part(ue_ref), late_part(ul_ref)], axis=0)
    labels = label_row(ue_ref, EARLY + LATE)
    _, own = weigh(unit, label_column(ue_ref, EARLY + LATE), unit, labels, False, True, own=0)
    own_ref[...] = own


def partner_kernel(ue_ref, ul_ref, xe_ref, xl_ref, own_in_ref, own_ref, x_labels_ref, copy_ref):
    copy_ref[...] = ul_ref[...]
    unit = jnp.concatenate([early_part(ue_ref), late_part(ul_ref)], axis=0)
    labels, x_labels = label_row(ue_ref, EARLY + LATE), label_column(xe_ref, EARLY + LATE)
    x_labels_ref[...] = x_labels
    _, a = weigh(early_part(xe_ref), x_labels[:EARLY], unit, labels, False, True)
    _, b = weigh(late_part(xl_ref), x_labels[EARLY:], unit, labels, False, True)
    own_ref[...] = own_in_ref[...] + a + b


def is_even():
    return lax.rem(lax.axis_index("blk"), 2) == 0


def is_lower():
    return lax.rem(lax.axis_index("blk"), LONG) < 2


def is_upper():
    return lax.rem(lax.axis_index("blk"), LONG) >= LONG - 2


def copy_when(condition, source_ref, out_ref):
    @pl.when(condition)
    def _():
        out_ref[...] = source_ref[...]


def pick_early_kernel(p_ref, n_ref, after_ref, out_ref):
    even = is_even()
    copy_when(even, n_ref, out_ref)
    copy_when(jnp.logical_not(even), p_ref, out_ref)


def pick_late_kernel(p_ref, n_ref, w_ref, after_ref, out_ref):
    even = is_even()
    odd = jnp.logical_not(even)
    copy_when(even & is_upper(), w_ref, out_ref)
    copy_when(even & jnp.logical_not(is_upper()), n_ref, out_ref)
    copy_when(odd & is_lower(), w_ref, out_ref)
    copy_when(odd & jnp.logical_not(is_lower()), p_ref, out_ref)


def labels_kernel(p_ref, after_ref, labels_ref):
    labels_ref[...] = label_column(p_ref, EARLY + LATE)


def early_kernel(
    ue_ref, ul_ref, xe_ref, xl_ref, pe_ref, ne_ref, x_labels_ref, own_in_ref,
    own_ref, p_ref, n_ref, n_labels_ref,
):
    n_labels = label_column(ne_ref, EARLY + LATE)
    n_labels_ref[...] = n_labels
    n, labels = early_part(ne_ref), n_labels[:EARLY]
    n1, own1 = weigh(n, labels, early_part(ue_ref), row_of(ue_ref, False), True, True)
    n2, own2 = weigh(n, labels, late_part(ul_ref), row_of(ue_ref, True), True, True)
    n3, p1 = weigh(n, labels, early_part(pe_ref), row_of(pe_ref, False), True, True)
    own_ref[:, :EARLY] = own_in_ref[:, :EARLY] + own1
    own_ref[:, EARLY:] = own_in_ref[:, EARLY:] + own2
    labels = row_of(ne_ref, False)
    _, n4 = weigh(early_part(xe_ref), x_labels_ref[:EARLY], n, labels, False, True)
    _, n5 = weigh(late_part(xl_ref), x_labels_ref[EARLY:], n, labels, False, True)
    n_ref[...] = n4 + n5 + add(n1, n2, n3)
    p, labels = early_part(pe_ref), row_of(pe_ref, False)
    _, p2 = weigh(early_part(xe_ref), x_labels_ref[:EARLY], p, labels, False, True)
    _, p3 = weigh(late_part(xl_ref), x_labels_ref[EARLY:], p, labels, False, True)
    p_ref[...] = p1 + p2 + p3


def early_f_kernel(fe_ref, re_ref, p_in_ref, n_in_ref, p_ref, n_ref, f_labels_ref):
    even = is_even()
    f_labels = label_column(fe_ref, EARLY + LATE)
    f_labels_ref[...] = f_labels
    _, more = weigh(early_part(fe_ref), f_labels[:EARLY], early_part(re_ref), row_of(re_ref, False), False, True)
    p_ref[...] = p_in_ref[...] + jnp.where(even, 0.0, more)
    n_ref[...] = n_in_ref[...] + jnp.where(even, more, 0.0)


def with_late_n(n_ref, ue_ref, ul_ref, xe_ref, xl_ref, pe_ref, ne_ref, n_labels_ref):
    n, labels = late_part(n_ref), n_labels_ref[EARLY:]
    n1, own1 = weigh(n, labels, early_part(ue_ref), row_of(ue_ref, False), True, True)
    n2, own2 = weigh(n, labels, late_part(ul_ref), row_of(ue_ref, True), True, True)
    n3, p1 = weigh(n, labels, early_part(pe_ref), row_of(pe_ref, False), True, True)
    n4, _ = weigh(n, labels, early_part(xe_ref), row_of(xe_ref, False), True, False)
    n5, _ = weigh(n, labels, late_part(xl_ref), row_of(xe_ref, True), True, False)
    return (n1, n2, n3, n4, n5), own1, own2, p1


def with_late_p(p_ref, xe_ref, xl_ref, pe_ref, ne_ref, p_labels_ref):
    p, labels = late_part(p_ref), p_labels_ref[EARLY:]
    p1, n1 = weigh(p, labels, early_part(ne_ref), row_of(ne_ref, False), True, True)
    p2, _ = weigh(p, labels, early_part(xe_ref), row_of(xe_ref, False), True, False)
    p3, _ = weigh(p, labels, late_part(xl_ref), row_of(xe_ref, True), True, False)
    return (p1, p2, p3), n1


def near_kernel(
    pl_ref, nl_ref, ue_ref, ul_ref, xe_ref, xl_ref, ne_ref, pe_ref, p_labels_ref, n_labels_ref,
    own_in_ref, p_in_ref, n_in_ref, own_ref, p_ref, n_ref, p_late_ref, n_late_ref,
):
    upper, lower = is_upper(), is_lower()
    copy_when(upper, own_in_ref, own_ref)
    copy_when(upper, p_in_ref, p_ref)
    copy_when(lower, n_in_ref, n_ref)

    @pl.when(jnp.logical_not(upper))
    def _():
        n, own1, own2, p1 = with_late_n(nl_ref, ue_ref, ul_ref, xe_ref, xl_ref, pe_ref, ne_ref, n_labels_ref)
        own_ref[:, :EARLY] = own_in_ref[:, :EARLY] + own1
        own_ref[:, EARLY:] = own_in_ref[:, EARLY:] + own2
        p_ref[...] = p_in_ref[...] + p1
        n_late_ref[...] = add(*n)

    @pl.when(jnp.logical_not(lower))
    def _():
        p, n1 = with_late_p(pl_ref, xe_ref, xl_ref, pe_ref, ne_ref, p_labels_ref)
        n_ref[...] = n_in_ref[...] + n1
        p_late_ref[...] = add(*p)


def far_kernel(
    w_ref, nl_ref, pl_ref, ue_ref, ul_ref, xe_ref, xl_ref, ne_ref, pe_ref, p_labels_ref, n_labels_ref,
    own_in_ref, p_in_ref, n_in_ref, p_late_ref, n_late_ref, fe_ref, re_ref, rl_ref, f_labels_ref,
    own_ref, p_ref, n_ref,
):
    upper, lower = is_upper(), is_lower()

    @pl.when(upper)
    def _():
        n, own1, own2, p1 = with_late_n(w_ref, ue_ref, ul_ref, xe_ref, xl_ref, pe_ref, ne_ref, n_labels_ref)
        labels = n_labels_ref[EARLY:]
        n6, p2 = weigh(late_part(w_ref), labels, late_part(pl_ref), row_of(pe_ref, True), True, True)
        own_ref[:, :EARLY] = own_in_ref[:, :EARLY] + own1
        own_ref[:, EARLY:] = own_in_ref[:, EARLY:] + own2
        p_ref[:, :EARLY] = p_in_ref[...] + p1
        p_ref[:, EARLY:] = p_late_ref[...] + p2
        n_ref[:, :EARLY] = n_in_ref[...]
        n_ref[:, EARLY:] = add(*n, n6)

    @pl.when(jnp.logical_not(upper))
    def _():
        own_ref[...] = own_in_ref[...]
        p_ref[:, :EARLY] = p_in_ref[...]

    @pl.when(lower)
    def _():
        p, n1 = with_late_p(w_ref, xe_ref, xl_ref, pe_ref, ne_ref, p_labels_ref)
        labels = p_labels_ref[EARLY:]
        p4, n2 = weigh(late_part(w_ref), labels, late_part(nl_ref), row_of(ne_ref, True), True, True)
        p_ref[:, EARLY:] = add(*p, p4)
        n_ref[:, :EARLY] = n_in_ref[...] + n1
        n_ref[:, EARLY:] = n_late_ref[...] + n2

    @pl.when(jnp.logical_not(lower | upper))
    def _():
        labels = p_labels_ref[EARLY:]
        p1, n1 = weigh(late_part(pl_ref), labels, late_part(nl_ref), row_of(ne_ref, True), True, True)
        p_ref[:, EARLY:] = p_late_ref[...] + add(p1)
        n_ref[:, :EARLY] = n_in_ref[...]
        n_ref[:, EARLY:] = n_late_ref[...] + n1

    @pl.when(is_even())
    def _():
        n_ref[:, EARLY:] = n_ref[:, EARLY:] + early_f_late(fe_ref, re_ref, rl_ref, f_labels_ref)


def early_f_late(fe_ref, re_ref, rl_ref, f_labels_ref):
    late = late_part(rl_ref)
    return weigh(early_part(fe_ref), f_labels_ref[:EARLY], late, row_of(re_ref, True), False, True)[1]


def late_f(fl_ref, re_ref, rl_ref, f_labels_ref):
    f, labels = late_part(fl_ref), f_labels_ref[EARLY:]
    _, a = weigh(f, labels, early_part(re_ref), row_of(re_ref, False), False, True)
    _, b = weigh(f, labels, late_part(rl_ref), row_of(re_ref, True), False, True)
    return a, b


def end_n_kernel(fl_ref, re_ref, rl_ref, f_labels_ref, n_in_ref, n_ref):
    copy_when(jnp.logical_not(is_even()), n_in_ref, n_ref)

    @pl.when(is_even())
    def _():
        a, b = late_f(fl_ref, re_ref, rl_ref, f_labels_ref)
        n_ref[...] = n_in_ref[...] + jnp.concatenate([a, b], axis=1)


def end_p_kernel(fe_ref, fl_ref, re_ref, rl_ref, f_labels_ref, p_in_ref, after_ref, p_ref):
    copy_when(is_even(), p_in_ref, p_ref)

    @pl.when(jnp.logical_not(is_even()))
    def _():
        a, b = late_f(fl_ref, re_ref, rl_ref, f_labels_ref)
        c = early_f_late(fe_ref, re_ref, rl_ref, f_labels_ref)
        p_ref[...] = p_in_ref[...] + jnp.concatenate([a, b + c], axis=1)


def sum_kernel(own_ref, more_ref, out_ref):
    out_ref[...] = own_ref[...] + more_ref[...]


def last_kernel(own_ref, more_ref, agreement_ref, log_ref):
    sums = own_ref[...] + more_ref[...]
    agreement = sums[1:2] / sums[0:1]
    log_weight = jnp.log(sums[0:1] * math.exp(-1.0 / TAU))
    for k in range(agreement_ref.shape[0]):
        agreement_ref[k : k + 1, :] = agreement[:, k * LANES : (k + 1) * LANES]
        log_ref[k : k + 1, :] = log_weight[:, k * LANES : (k + 1) * LANES]


def on_device(embeddings, labels):
    n, depth = embeddings.shape
    slabs = depth // LANES
    size = lax.axis_size("blk")
    up = [(i, (i + 2) % size) for i in range(size)]
    down = [(i, (i - 2) % size) for i in range(size)]
    swap = [(i, i ^ 1) for i in range(size)]
    send = lambda array, route: lax.ppermute(array, "blk", route)
    struct = jax.ShapeDtypeStruct
    sums, early_sums = struct((2, n), F32), struct((2, EARLY), F32)
    early, late = struct((HEAD + slabs * EARLY, LANES), BF16), struct((slabs * LATE, LANES), BF16)

    hbm = pl.BlockSpec(memory_space=pltpu.HBM)
    labels = pltpu.with_memory_space_constraint(labels.reshape(n // LANES, LANES), pltpu.HBM)
    ue = call(
        unit_early_kernel,
        early,
        (embeddings, labels),
        "unit_early",
        0.1,
        in_specs=[hbm, hbm],
        scratch=[
            pltpu.VMEM((EARLY, depth), F32),
            pltpu.VMEM((n // LANES, LANES), jnp.int32),
            pltpu.SemaphoreType.DMA((2,)),
            pltpu.SemaphoreType.DMA,
        ],
        limit=52,
    )
    ul = call(
        unit_late_kernel,
        late,
        (embeddings, ue),
        "unit_late",
        0.1,
        in_specs=[hbm, pl.BlockSpec(memory_space=pltpu.VMEM)],
        scratch=[pltpu.VMEM((LATE, depth), F32), pltpu.SemaphoreType.DMA((2,))],
        limit=52,
    )
    pe = send(ue, up)
    ne = send(ue, down)
    xe = send(lax.optimization_barrier((ue, ul))[0], swap)
    xl = send(ul, swap)
    own = call(own_kernel, sums, (ue, ul), "own", 1)
    column, late_sums = struct((n, LANES), F32), struct((2, LATE), F32)
    own, x_labels, copy = call(partner_kernel, (sums, column, late), (ue, ul, xe, xl, own), "with_partner", 1)
    upper = [i for i in range(size) if i % LONG >= LONG - 2]
    far = [(i, (i + 2) % size) for i in upper] + [((i + 2) % size, i) for i in upper]
    late_p = send(copy, [pair for pair in up if pair not in far])
    late_n = send(copy, [pair for pair in down if pair not in far])
    late_w = send(copy, far)

    p_labels = call(labels_kernel, column, (pe, own), "labels", 0.1)
    re = call(pick_early_kernel, early, (pe, ne, p_labels), "pick", 0.1)
    fe = send(re, swap)
    own, p, q, q_labels = call(
        early_kernel,
        (sums, early_sums, early_sums, column),
        (ue, ul, xe, xl, pe, ne, x_labels, own),
        "early",
        2.5,
    )
    p, q, f_labels = call(early_f_kernel, (early_sums, early_sums, column), (fe, re, p, q), "early_f", 0.5)
    fixed = (ue, ul, xe, xl, ne, pe, p_labels, q_labels)
    own, p, q, p_late, q_late = call(
        near_kernel,
        (sums, early_sums, early_sums, late_sums, late_sums),
        (late_p, late_n, *fixed, own, p, q),
        "near",
        1.7,
    )
    rl = call(pick_late_kernel, late, (late_p, late_n, late_w, q), "pick_late", 0.1)
    fl = send(rl, swap)
    own, p, q = call(
        far_kernel,
        (sums, sums, sums),
        (late_w, late_n, late_p, *fixed, own, p, q, p_late, q_late, fe, re, rl, f_labels),
        "far",
        0.2,
    )
    q = call(end_n_kernel, sums, (fl, re, rl, f_labels, q), "end_n", 0.3)
    from_lower = send(q, up)
    p = call(end_p_kernel, sums, (fe, fl, re, rl, f_labels, p, q), "end_p", 0.3)
    from_upper = send(p, down)
    own = call(sum_kernel, sums, (own, from_lower), "sum", 0.001)
    shape = struct((n // LANES, LANES), F32)
    agreement, log_weight = call(last_kernel, (shape, shape), (own, from_upper), "last", 0.01)
    return agreement.reshape(n), log_weight.reshape(n)


def solution(mesh):
    return jax.shard_map(
        on_device,
        mesh=mesh,
        in_specs=(P("blk", None), P("blk")),
        out_specs=(P("blk"), P("blk")),
        check_vma=False,
    )
```

```python
import functools
import math

import jax
import jax.numpy as jnp
from jax import lax
from jax.experimental import pallas as pl
from jax.experimental.pallas import tpu as pltpu
from jax.sharding import PartitionSpec as P

TAU = 0.1
SCALE = math.log2(math.e) / TAU
LANES = 128
HEAD = 16
EARLY = 512
LATE = 256
CHUNK = 512
LONG = 8
STEP = 256
F32 = jnp.float32
BF16 = jnp.bfloat16


def call(kernel, out_shape, operands, name, tiles, in_specs=None, scratch=(), limit=28):
    vmem = pl.BlockSpec(memory_space=pltpu.VMEM)
    return pl.pallas_call(
        kernel,
        out_shape=out_shape,
        in_specs=in_specs or [vmem] * len(operands),
        out_specs=jax.tree.map(lambda _: vmem, out_shape),
        scratch_shapes=scratch,
        name=name,
        cost_estimate=pl.CostEstimate(
            flops=int(1.2e10 * tiles),
            bytes_accessed=1024,
            transcendentals=0,
        ),
        compiler_params=pltpu.CompilerParams(vmem_limit_bytes=limit * 1024 * 1024),
    )(*operands)


def images(ref, n, first, count, head=HEAD):
    slabs = (ref.shape[0] - head) // n
    return jnp.concatenate(
        [ref[head + k * n + first : head + k * n + first + count, :] for k in range(slabs)], axis=1
    )


def label_row(ref, n):
    head = ref[0:HEAD, :].astype(F32)
    groups = n // LANES
    return jnp.concatenate([head[k : k + 1] + head[k + groups : k + groups + 1] for k in range(groups)], axis=1)


def label_column(ref, n):
    groups = n // LANES
    row = lax.broadcasted_iota(jnp.int32, (HEAD, n), 0)
    group = lax.broadcasted_iota(jnp.int32, (HEAD, n), 1) // LANES
    pick = jnp.where((row == group) | (row == group + groups), 1.0, 0.0).astype(BF16)
    spread = lax.dot_general(ref[0:HEAD, :], pick, (((0,), (0,)), ((), ())), preferred_element_type=F32)
    return jnp.concatenate([spread[:, k * LANES : (k + 1) * LANES] for k in range(groups)], axis=0)


def along_lanes(partial):
    return jnp.concatenate(
        [
            jnp.sum(partial[i : i + LANES].T, axis=0, keepdims=True)
            for i in range(0, partial.shape[0], LANES)
        ],
        axis=1,
    )


def weigh(left, left_labels, right, right_labels, rows, columns, own=None):
    m, n = left.shape[0], right.shape[0]
    row_parts, column = [], None
    for i in range(0, m, CHUNK):
        chunk = min(CHUNK, m - i)
        here = left[i : i + chunk]
        labels = jnp.concatenate([left_labels[i : i + chunk]] * (STEP // LANES), axis=1)
        totals, sames, row_total, row_same = [], [], None, None
        for j in range(0, n, STEP):
            score = lax.dot_general(
                here, right[j : j + STEP], (((1,), (1,)), ((), ())), preferred_element_type=F32
            )
            weight = jnp.exp2(score * SCALE)
            if own is not None:
                r = lax.broadcasted_iota(jnp.int32, (chunk, STEP), 0) + (own + i)
                c = lax.broadcasted_iota(jnp.int32, (chunk, STEP), 1) + j
                weight = jnp.where(r == c, 0.0, weight)
            same = jnp.where(labels == right_labels[:, j : j + STEP], weight, 0.0)
            if rows:
                for k in range(0, STEP, LANES):
                    a, b = weight[:, k : k + LANES], same[:, k : k + LANES]
                    row_total = a if row_total is None else row_total + a
                    row_same = b if row_same is None else row_same + b
            if columns:
                totals.append(jnp.sum(weight, axis=0, keepdims=True))
                sames.append(jnp.sum(same, axis=0, keepdims=True))
        if rows:
            row_parts.append((row_total, row_same))
        if columns:
            both = jnp.concatenate([jnp.concatenate(totals, axis=1), jnp.concatenate(sames, axis=1)], axis=0)
            column = both if column is None else column + both
    rows_out = tuple(jnp.concatenate(p, axis=0) for p in zip(*row_parts)) if rows else None
    return rows_out, column


def add(*pairs):
    total, same = pairs[0]
    for more_total, more_same in pairs[1:]:
        total, same = total + more_total, same + more_same
    return jnp.concatenate([along_lanes(total), along_lanes(same)], axis=0)


def early_part(ref):
    return images(ref, EARLY, 0, EARLY)


def late_part(ref):
    return images(ref, LATE, 0, LATE, head=0)


def row_of(early_ref, late):
    row = label_row(early_ref, EARLY + LATE)
    return row[:, EARLY:] if late else row[:, :EARLY]


def normalise(x_ref, first, held, sems, write):
    rows, parts = held.shape[0], sems.shape[0]
    part = rows // parts
    copies = [
        pltpu.make_async_copy(
            x_ref.at[pl.ds(first + i * part, part), :], held.at[pl.ds(i * part, part), :], sems.at[i]
        )
        for i in range(parts)
    ]
    for copy in copies:
        copy.start()
    for i in range(parts):
        copies[i].wait()
        x = held[i * part : (i + 1) * part, :]
        unit = (x * lax.rsqrt(jnp.sum(x * x, axis=1, keepdims=True) + 1e-06)).astype(BF16)
        for k in range(x.shape[1] // LANES):
            write(k, i * part, unit[:, k * LANES : (k + 1) * LANES])


def unit_early_kernel(x_ref, labels_hbm, out_ref, held, labels_ref, sems, labels_sem):
    labels_copy = pltpu.make_async_copy(labels_hbm, labels_ref, labels_sem)
    labels_copy.start()

    def write(slab, row, unit):
        out_ref[HEAD + slab * EARLY + row : HEAD + slab * EARLY + row + unit.shape[0], :] = unit

    normalise(x_ref, 0, held, sems, write)
    labels_copy.wait()
    labels = labels_ref[...]
    low = lax.rem(labels, 256)
    blank = jnp.zeros((HEAD - 2 * labels.shape[0], LANES), F32)
    head = jnp.concatenate([(labels - low).astype(F32), low.astype(F32), blank], axis=0)
    out_ref[0:HEAD, :] = head.astype(BF16)


def unit_late_kernel(x_ref, after_ref, out_ref, held, sems):
    def write(slab, row, unit):
        out_ref[slab * LATE + row : slab * LATE + row + unit.shape[0], :] = unit

    normalise(x_ref, EARLY, held, sems, write)


def own_kernel(ue_ref, ul_ref, own_ref):
    unit = jnp.concatenate([early_part(ue_ref), late_part(ul_ref)], axis=0)
    labels = label_row(ue_ref, EARLY + LATE)
    _, own = weigh(unit, label_column(ue_ref, EARLY + LATE), unit, labels, False, True, own=0)
    own_ref[...] = own


def partner_kernel(ue_ref, ul_ref, xe_ref, xl_ref, own_in_ref, own_ref, x_labels_ref, copy_ref):
    copy_ref[...] = ul_ref[...]
    unit = jnp.concatenate([early_part(ue_ref), late_part(ul_ref)], axis=0)
    labels, x_labels = label_row(ue_ref, EARLY + LATE), label_column(xe_ref, EARLY + LATE)
    x_labels_ref[...] = x_labels
    _, a = weigh(early_part(xe_ref), x_labels[:EARLY], unit, labels, False, True)
    _, b = weigh(late_part(xl_ref), x_labels[EARLY:], unit, labels, False, True)
    own_ref[...] = own_in_ref[...] + a + b


def is_even():
    return lax.rem(lax.axis_index("blk"), 2) == 0


def is_lower():
    return lax.rem(lax.axis_index("blk"), LONG) < 2


def is_upper():
    return lax.rem(lax.axis_index("blk"), LONG) >= LONG - 2


def copy_when(condition, source_ref, out_ref):
    @pl.when(condition)
    def _():
        out_ref[...] = source_ref[...]


def pick_early_kernel(p_ref, n_ref, after_ref, out_ref):
    even = is_even()
    copy_when(even, n_ref, out_ref)
    copy_when(jnp.logical_not(even), p_ref, out_ref)


def pick_late_kernel(p_ref, n_ref, w_ref, after_ref, out_ref):
    even = is_even()
    odd = jnp.logical_not(even)
    copy_when(even & is_upper(), w_ref, out_ref)
    copy_when(even & jnp.logical_not(is_upper()), n_ref, out_ref)
    copy_when(odd & is_lower(), w_ref, out_ref)
    copy_when(odd & jnp.logical_not(is_lower()), p_ref, out_ref)


def labels_kernel(p_ref, after_ref, labels_ref):
    labels_ref[...] = label_column(p_ref, EARLY + LATE)


def early_kernel(
    ue_ref, ul_ref, xe_ref, xl_ref, pe_ref, ne_ref, x_labels_ref, own_in_ref,
    own_ref, p_ref, n_ref, n_labels_ref,
):
    n_labels = label_column(ne_ref, EARLY + LATE)
    n_labels_ref[...] = n_labels
    n, labels = early_part(ne_ref), n_labels[:EARLY]
    n1, own1 = weigh(n, labels, early_part(ue_ref), row_of(ue_ref, False), True, True)
    n2, own2 = weigh(n, labels, late_part(ul_ref), row_of(ue_ref, True), True, True)
    n3, p1 = weigh(n, labels, early_part(pe_ref), row_of(pe_ref, False), True, True)
    own_ref[:, :EARLY] = own_in_ref[:, :EARLY] + own1
    own_ref[:, EARLY:] = own_in_ref[:, EARLY:] + own2
    labels = row_of(ne_ref, False)
    _, n4 = weigh(early_part(xe_ref), x_labels_ref[:EARLY], n, labels, False, True)
    _, n5 = weigh(late_part(xl_ref), x_labels_ref[EARLY:], n, labels, False, True)
    n_ref[...] = n4 + n5 + add(n1, n2, n3)
    p, labels = early_part(pe_ref), row_of(pe_ref, False)
    _, p2 = weigh(early_part(xe_ref), x_labels_ref[:EARLY], p, labels, False, True)
    _, p3 = weigh(late_part(xl_ref), x_labels_ref[EARLY:], p, labels, False, True)
    p_ref[...] = p1 + p2 + p3


def early_f_kernel(fe_ref, re_ref, p_in_ref, n_in_ref, p_ref, n_ref, f_labels_ref):
    even = is_even()
    f_labels = label_column(fe_ref, EARLY + LATE)
    f_labels_ref[...] = f_labels
    _, more = weigh(early_part(fe_ref), f_labels[:EARLY], early_part(re_ref), row_of(re_ref, False), False, True)
    p_ref[...] = p_in_ref[...] + jnp.where(even, 0.0, more)
    n_ref[...] = n_in_ref[...] + jnp.where(even, more, 0.0)


def with_late_n(n_ref, ue_ref, ul_ref, xe_ref, xl_ref, pe_ref, ne_ref, n_labels_ref):
    n, labels = late_part(n_ref), n_labels_ref[EARLY:]
    n1, own1 = weigh(n, labels, early_part(ue_ref), row_of(ue_ref, False), True, True)
    n2, own2 = weigh(n, labels, late_part(ul_ref), row_of(ue_ref, True), True, True)
    n3, p1 = weigh(n, labels, early_part(pe_ref), row_of(pe_ref, False), True, True)
    n4, _ = weigh(n, labels, early_part(xe_ref), row_of(xe_ref, False), True, False)
    n5, _ = weigh(n, labels, late_part(xl_ref), row_of(xe_ref, True), True, False)
    return (n1, n2, n3, n4, n5), own1, own2, p1


def with_late_p(p_ref, xe_ref, xl_ref, pe_ref, ne_ref, p_labels_ref):
    p, labels = late_part(p_ref), p_labels_ref[EARLY:]
    p1, n1 = weigh(p, labels, early_part(ne_ref), row_of(ne_ref, False), True, True)
    p2, _ = weigh(p, labels, early_part(xe_ref), row_of(xe_ref, False), True, False)
    p3, _ = weigh(p, labels, late_part(xl_ref), row_of(xe_ref, True), True, False)
    return (p1, p2, p3), n1


def near_kernel(
    pl_ref, nl_ref, ue_ref, ul_ref, xe_ref, xl_ref, ne_ref, pe_ref, p_labels_ref, n_labels_ref,
    own_in_ref, p_in_ref, n_in_ref, own_ref, p_ref, n_ref, p_late_ref, n_late_ref,
):
    upper, lower = is_upper(), is_lower()
    copy_when(upper, own_in_ref, own_ref)
    copy_when(upper, p_in_ref, p_ref)
    copy_when(lower, n_in_ref, n_ref)

    @pl.when(jnp.logical_not(upper))
    def _():
        n, own1, own2, p1 = with_late_n(nl_ref, ue_ref, ul_ref, xe_ref, xl_ref, pe_ref, ne_ref, n_labels_ref)
        own_ref[:, :EARLY] = own_in_ref[:, :EARLY] + own1
        own_ref[:, EARLY:] = own_in_ref[:, EARLY:] + own2
        p_ref[...] = p_in_ref[...] + p1
        n_late_ref[...] = add(*n)

    @pl.when(jnp.logical_not(lower))
    def _():
        p, n1 = with_late_p(pl_ref, xe_ref, xl_ref, pe_ref, ne_ref, p_labels_ref)
        n_ref[...] = n_in_ref[...] + n1
        p_late_ref[...] = add(*p)


def far_kernel(
    w_ref, nl_ref, pl_ref, ue_ref, ul_ref, xe_ref, xl_ref, ne_ref, pe_ref, p_labels_ref, n_labels_ref,
    own_in_ref, p_in_ref, n_in_ref, p_late_ref, n_late_ref, fe_ref, re_ref, rl_ref, f_labels_ref,
    own_ref, p_ref, n_ref,
):
    upper, lower = is_upper(), is_lower()

    @pl.when(upper)
    def _():
        n, own1, own2, p1 = with_late_n(w_ref, ue_ref, ul_ref, xe_ref, xl_ref, pe_ref, ne_ref, n_labels_ref)
        labels = n_labels_ref[EARLY:]
        n6, p2 = weigh(late_part(w_ref), labels, late_part(pl_ref), row_of(pe_ref, True), True, True)
        own_ref[:, :EARLY] = own_in_ref[:, :EARLY] + own1
        own_ref[:, EARLY:] = own_in_ref[:, EARLY:] + own2
        p_ref[:, :EARLY] = p_in_ref[...] + p1
        p_ref[:, EARLY:] = p_late_ref[...] + p2
        n_ref[:, :EARLY] = n_in_ref[...]
        n_ref[:, EARLY:] = add(*n, n6)

    @pl.when(jnp.logical_not(upper))
    def _():
        own_ref[...] = own_in_ref[...]
        p_ref[:, :EARLY] = p_in_ref[...]

    @pl.when(lower)
    def _():
        p, n1 = with_late_p(w_ref, xe_ref, xl_ref, pe_ref, ne_ref, p_labels_ref)
        labels = p_labels_ref[EARLY:]
        p4, n2 = weigh(late_part(w_ref), labels, late_part(nl_ref), row_of(ne_ref, True), True, True)
        p_ref[:, EARLY:] = add(*p, p4)
        n_ref[:, :EARLY] = n_in_ref[...] + n1
        n_ref[:, EARLY:] = n_late_ref[...] + n2

    @pl.when(jnp.logical_not(lower | upper))
    def _():
        labels = p_labels_ref[EARLY:]
        p1, n1 = weigh(late_part(pl_ref), labels, late_part(nl_ref), row_of(ne_ref, True), True, True)
        p_ref[:, EARLY:] = p_late_ref[...] + add(p1)
        n_ref[:, :EARLY] = n_in_ref[...]
        n_ref[:, EARLY:] = n_late_ref[...] + n1

    @pl.when(is_even())
    def _():
        n_ref[:, EARLY:] = n_ref[:, EARLY:] + early_f_late(fe_ref, re_ref, rl_ref, f_labels_ref)


def early_f_late(fe_ref, re_ref, rl_ref, f_labels_ref):
    late = late_part(rl_ref)
    return weigh(early_part(fe_ref), f_labels_ref[:EARLY], late, row_of(re_ref, True), False, True)[1]


def late_f(fl_ref, re_ref, rl_ref, f_labels_ref):
    f, labels = late_part(fl_ref), f_labels_ref[EARLY:]
    _, a = weigh(f, labels, early_part(re_ref), row_of(re_ref, False), False, True)
    _, b = weigh(f, labels, late_part(rl_ref), row_of(re_ref, True), False, True)
    return a, b


def end_n_kernel(fl_ref, re_ref, rl_ref, f_labels_ref, n_in_ref, n_ref):
    copy_when(jnp.logical_not(is_even()), n_in_ref, n_ref)

    @pl.when(is_even())
    def _():
        a, b = late_f(fl_ref, re_ref, rl_ref, f_labels_ref)
        n_ref[...] = n_in_ref[...] + jnp.concatenate([a, b], axis=1)


def end_p_kernel(fe_ref, fl_ref, re_ref, rl_ref, f_labels_ref, p_in_ref, after_ref, p_ref):
    copy_when(is_even(), p_in_ref, p_ref)

    @pl.when(jnp.logical_not(is_even()))
    def _():
        a, b = late_f(fl_ref, re_ref, rl_ref, f_labels_ref)
        c = early_f_late(fe_ref, re_ref, rl_ref, f_labels_ref)
        p_ref[...] = p_in_ref[...] + jnp.concatenate([a, b + c], axis=1)


def sum_kernel(own_ref, more_ref, out_ref):
    out_ref[...] = own_ref[...] + more_ref[...]


def last_kernel(own_ref, more_ref, agreement_ref, log_ref):
    sums = own_ref[...] + more_ref[...]
    agreement = sums[1:2] / sums[0:1]
    log_weight = jnp.log(sums[0:1] * math.exp(-1.0 / TAU))
    for k in range(agreement_ref.shape[0]):
        agreement_ref[k : k + 1, :] = agreement[:, k * LANES : (k + 1) * LANES]
        log_ref[k : k + 1, :] = log_weight[:, k * LANES : (k + 1) * LANES]


def on_device(embeddings, labels):
    n, depth = embeddings.shape
    slabs = depth // LANES
    size = lax.axis_size("blk")
    up = [(i, (i + 2) % size) for i in range(size)]
    down = [(i, (i - 2) % size) for i in range(size)]
    swap = [(i, i ^ 1) for i in range(size)]
    send = lambda array, route: lax.ppermute(array, "blk", route)
    struct = jax.ShapeDtypeStruct
    sums, early_sums = struct((2, n), F32), struct((2, EARLY), F32)
    early, late = struct((HEAD + slabs * EARLY, LANES), BF16), struct((slabs * LATE, LANES), BF16)

    hbm = pl.BlockSpec(memory_space=pltpu.HBM)
    labels = pltpu.with_memory_space_constraint(labels.reshape(n // LANES, LANES), pltpu.HBM)
    ue = call(
        unit_early_kernel,
        early,
        (embeddings, labels),
        "unit_early",
        0.1,
        in_specs=[hbm, hbm],
        scratch=[
            pltpu.VMEM((EARLY, depth), F32),
            pltpu.VMEM((n // LANES, LANES), jnp.int32),
            pltpu.SemaphoreType.DMA((4,)),
            pltpu.SemaphoreType.DMA,
        ],
        limit=52,
    )
    ul = call(
        unit_late_kernel,
        late,
        (embeddings, ue),
        "unit_late",
        0.1,
        in_specs=[hbm, pl.BlockSpec(memory_space=pltpu.VMEM)],
        scratch=[pltpu.VMEM((LATE, depth), F32), pltpu.SemaphoreType.DMA((2,))],
        limit=52,
    )
    pe = send(ue, up)
    ne = send(ue, down)
    xe = send(lax.optimization_barrier((ue, ul))[0], swap)
    xl = send(ul, swap)
    own = call(own_kernel, sums, (ue, ul), "own", 1)
    column, late_sums = struct((n, LANES), F32), struct((2, LATE), F32)
    own, x_labels, copy = call(partner_kernel, (sums, column, late), (ue, ul, xe, xl, own), "with_partner", 1)
    upper = [i for i in range(size) if i % LONG >= LONG - 2]
    far = [(i, (i + 2) % size) for i in upper] + [((i + 2) % size, i) for i in upper]
    late_p = send(copy, [pair for pair in up if pair not in far])
    late_n = send(copy, [pair for pair in down if pair not in far])
    late_w = send(copy, far)

    p_labels = call(labels_kernel, column, (pe, own), "labels", 0.1)
    re = call(pick_early_kernel, early, (pe, ne, p_labels), "pick", 0.1)
    fe = send(re, swap)
    own, p, q, q_labels = call(
        early_kernel,
        (sums, early_sums, early_sums, column),
        (ue, ul, xe, xl, pe, ne, x_labels, own),
        "early",
        2.5,
    )
    p, q, f_labels = call(early_f_kernel, (early_sums, early_sums, column), (fe, re, p, q), "early_f", 0.5)
    fixed = (ue, ul, xe, xl, ne, pe, p_labels, q_labels)
    own, p, q, p_late, q_late = call(
        near_kernel,
        (sums, early_sums, early_sums, late_sums, late_sums),
        (late_p, late_n, *fixed, own, p, q),
        "near",
        1.7,
    )
    rl = call(pick_late_kernel, late, (late_p, late_n, late_w, q), "pick_late", 0.1)
    fl = send(rl, swap)
    own, p, q = call(
        far_kernel,
        (sums, sums, sums),
        (late_w, late_n, late_p, *fixed, own, p, q, p_late, q_late, fe, re, rl, f_labels),
        "far",
        0.2,
    )
    q = call(end_n_kernel, sums, (fl, re, rl, f_labels, q), "end_n", 0.3)
    from_lower = send(q, up)
    p = call(end_p_kernel, sums, (fe, fl, re, rl, f_labels, p, q), "end_p", 0.3)
    from_upper = send(p, down)
    own = call(sum_kernel, sums, (own, from_lower), "sum", 0.001)
    shape = struct((n // LANES, LANES), F32)
    agreement, log_weight = call(last_kernel, (shape, shape), (own, from_upper), "last", 0.01)
    return agreement.reshape(n), log_weight.reshape(n)


def solution(mesh):
    return jax.shard_map(
        on_device,
        mesh=mesh,
        in_specs=(P("blk", None), P("blk")),
        out_specs=(P("blk"), P("blk")),
        check_vma=False,
    )
```

```python
import functools
import math

import jax
import jax.numpy as jnp
from jax import lax
from jax.experimental import pallas as pl
from jax.experimental.pallas import tpu as pltpu
from jax.sharding import PartitionSpec as P

TAU = 0.1
SCALE = math.log2(math.e) / TAU
LANES = 128
HEAD = 16
EARLY = 512
LATE = 256
CHUNK = 512
LONG = 8
STEP = 256
F32 = jnp.float32
BF16 = jnp.bfloat16


def call(kernel, out_shape, operands, name, tiles, in_specs=None, scratch=(), limit=28):
    vmem = pl.BlockSpec(memory_space=pltpu.VMEM)
    return pl.pallas_call(
        kernel,
        out_shape=out_shape,
        in_specs=in_specs or [vmem] * len(operands),
        out_specs=jax.tree.map(lambda _: vmem, out_shape),
        scratch_shapes=scratch,
        name=name,
        cost_estimate=pl.CostEstimate(
            flops=int(1.2e10 * tiles),
            bytes_accessed=1024,
            transcendentals=0,
        ),
        compiler_params=pltpu.CompilerParams(vmem_limit_bytes=limit * 1024 * 1024),
    )(*operands)


def images(ref, n, first, count, head=HEAD):
    slabs = (ref.shape[0] - head) // n
    return jnp.concatenate(
        [ref[head + k * n + first : head + k * n + first + count, :] for k in range(slabs)], axis=1
    )


def label_row(ref, n):
    head = ref[0:HEAD, :].astype(F32)
    groups = n // LANES
    return jnp.concatenate([head[k : k + 1] + head[k + groups : k + groups + 1] for k in range(groups)], axis=1)


def label_column(ref, n):
    groups = n // LANES
    row = lax.broadcasted_iota(jnp.int32, (HEAD, n), 0)
    group = lax.broadcasted_iota(jnp.int32, (HEAD, n), 1) // LANES
    pick = jnp.where((row == group) | (row == group + groups), 1.0, 0.0).astype(BF16)
    spread = lax.dot_general(ref[0:HEAD, :], pick, (((0,), (0,)), ((), ())), preferred_element_type=F32)
    return jnp.concatenate([spread[:, k * LANES : (k + 1) * LANES] for k in range(groups)], axis=0)


def along_lanes(partial):
    return jnp.concatenate(
        [
            jnp.sum(partial[i : i + LANES].T, axis=0, keepdims=True)
            for i in range(0, partial.shape[0], LANES)
        ],
        axis=1,
    )


def weigh(left, left_labels, right, right_labels, rows, columns, own=None):
    m, n = left.shape[0], right.shape[0]
    row_parts, column = [], None
    for i in range(0, m, CHUNK):
        chunk = min(CHUNK, m - i)
        here = left[i : i + chunk]
        labels = jnp.concatenate([left_labels[i : i + chunk]] * (STEP // LANES), axis=1)
        totals, sames, row_total, row_same = [], [], None, None
        for j in range(0, n, STEP):
            score = lax.dot_general(
                here, right[j : j + STEP], (((1,), (1,)), ((), ())), preferred_element_type=F32
            )
            weight = jnp.exp2(score * SCALE)
            if own is not None:
                r = lax.broadcasted_iota(jnp.int32, (chunk, STEP), 0) + (own + i)
                c = lax.broadcasted_iota(jnp.int32, (chunk, STEP), 1) + j
                weight = jnp.where(r == c, 0.0, weight)
            same = jnp.where(labels == right_labels[:, j : j + STEP], weight, 0.0)
            if rows:
                for k in range(0, STEP, LANES):
                    a, b = weight[:, k : k + LANES], same[:, k : k + LANES]
                    row_total = a if row_total is None else row_total + a
                    row_same = b if row_same is None else row_same + b
            if columns:
                totals.append(jnp.sum(weight, axis=0, keepdims=True))
                sames.append(jnp.sum(same, axis=0, keepdims=True))
        if rows:
            row_parts.append((row_total, row_same))
        if columns:
            both = jnp.concatenate([jnp.concatenate(totals, axis=1), jnp.concatenate(sames, axis=1)], axis=0)
            column = both if column is None else column + both
    rows_out = tuple(jnp.concatenate(p, axis=0) for p in zip(*row_parts)) if rows else None
    return rows_out, column


def add(*pairs):
    total, same = pairs[0]
    for more_total, more_same in pairs[1:]:
        total, same = total + more_total, same + more_same
    return jnp.concatenate([along_lanes(total), along_lanes(same)], axis=0)


def early_part(ref):
    return images(ref, EARLY, 0, EARLY)


def late_part(ref):
    return images(ref, LATE, 0, LATE, head=0)


def row_of(early_ref, late):
    row = label_row(early_ref, EARLY + LATE)
    return row[:, EARLY:] if late else row[:, :EARLY]


def normalise(x_ref, first, held, sems, write, meanwhile=None):
    rows, parts = held.shape[0], sems.shape[0]
    part = rows // parts
    copies = [
        pltpu.make_async_copy(
            x_ref.at[pl.ds(first + i * part, part), :], held.at[pl.ds(i * part, part), :], sems.at[i]
        )
        for i in range(parts)
    ]
    for copy in copies:
        copy.start()
    if meanwhile is not None:
        meanwhile()
    for i in range(parts):
        copies[i].wait()
        x = held[i * part : (i + 1) * part, :]
        unit = (x * lax.rsqrt(jnp.sum(x * x, axis=1, keepdims=True) + 1e-06)).astype(BF16)
        for k in range(x.shape[1] // LANES):
            write(k, i * part, unit[:, k * LANES : (k + 1) * LANES])


def unit_early_kernel(x_ref, labels_hbm, out_ref, held, labels_ref, sems, labels_sem):
    labels_copy = pltpu.make_async_copy(labels_hbm, labels_ref, labels_sem)
    labels_copy.start()

    def write(slab, row, unit):
        out_ref[HEAD + slab * EARLY + row : HEAD + slab * EARLY + row + unit.shape[0], :] = unit

    def write_labels():
        labels_copy.wait()
        labels = labels_ref[...]
        low = lax.rem(labels, 256)
        blank = jnp.zeros((HEAD - 2 * labels.shape[0], LANES), F32)
        head = jnp.concatenate([(labels - low).astype(F32), low.astype(F32), blank], axis=0)
        out_ref[0:HEAD, :] = head.astype(BF16)

    normalise(x_ref, 0, held, sems, write, write_labels)


def unit_late_kernel(x_ref, after_ref, out_ref, held, sems):
    def write(slab, row, unit):
        out_ref[slab * LATE + row : slab * LATE + row + unit.shape[0], :] = unit

    normalise(x_ref, EARLY, held, sems, write)


def own_kernel(ue_ref, ul_ref, own_ref):
    unit = jnp.concatenate([early_part(ue_ref), late_part(ul_ref)], axis=0)
    labels = label_row(ue_ref, EARLY + LATE)
    _, own = weigh(unit, label_column(ue_ref, EARLY + LATE), unit, labels, False, True, own=0)
    own_ref[...] = own


def partner_kernel(ue_ref, ul_ref, xe_ref, xl_ref, own_in_ref, own_ref, x_labels_ref, copy_ref):
    copy_ref[...] = ul_ref[...]
    unit = jnp.concatenate([early_part(ue_ref), late_part(ul_ref)], axis=0)
    labels, x_labels = label_row(ue_ref, EARLY + LATE), label_column(xe_ref, EARLY + LATE)
    x_labels_ref[...] = x_labels
    _, a = weigh(early_part(xe_ref), x_labels[:EARLY], unit, labels, False, True)
    _, b = weigh(late_part(xl_ref), x_labels[EARLY:], unit, labels, False, True)
    own_ref[...] = own_in_ref[...] + a + b


def is_even():
    return lax.rem(lax.axis_index("blk"), 2) == 0


def is_lower():
    return lax.rem(lax.axis_index("blk"), LONG) < 2


def is_upper():
    return lax.rem(lax.axis_index("blk"), LONG) >= LONG - 2


def copy_when(condition, source_ref, out_ref):
    @pl.when(condition)
    def _():
        out_ref[...] = source_ref[...]


def pick_early_kernel(p_ref, n_ref, after_ref, out_ref):
    even = is_even()
    copy_when(even, n_ref, out_ref)
    copy_when(jnp.logical_not(even), p_ref, out_ref)


def pick_late_kernel(p_ref, n_ref, w_ref, after_ref, out_ref):
    even = is_even()
    odd = jnp.logical_not(even)
    copy_when(even & is_upper(), w_ref, out_ref)
    copy_when(even & jnp.logical_not(is_upper()), n_ref, out_ref)
    copy_when(odd & is_lower(), w_ref, out_ref)
    copy_when(odd & jnp.logical_not(is_lower()), p_ref, out_ref)


def labels_kernel(p_ref, after_ref, labels_ref):
    labels_ref[...] = label_column(p_ref, EARLY + LATE)


def early_kernel(
    ue_ref, ul_ref, xe_ref, xl_ref, pe_ref, ne_ref, x_labels_ref, own_in_ref,
    own_ref, p_ref, n_ref, n_labels_ref,
):
    n_labels = label_column(ne_ref, EARLY + LATE)
    n_labels_ref[...] = n_labels
    n, labels = early_part(ne_ref), n_labels[:EARLY]
    n1, own1 = weigh(n, labels, early_part(ue_ref), row_of(ue_ref, False), True, True)
    n2, own2 = weigh(n, labels, late_part(ul_ref), row_of(ue_ref, True), True, True)
    n3, p1 = weigh(n, labels, early_part(pe_ref), row_of(pe_ref, False), True, True)
    own_ref[:, :EARLY] = own_in_ref[:, :EARLY] + own1
    own_ref[:, EARLY:] = own_in_ref[:, EARLY:] + own2
    labels = row_of(ne_ref, False)
    _, n4 = weigh(early_part(xe_ref), x_labels_ref[:EARLY], n, labels, False, True)
    _, n5 = weigh(late_part(xl_ref), x_labels_ref[EARLY:], n, labels, False, True)
    n_ref[...] = n4 + n5 + add(n1, n2, n3)
    p, labels = early_part(pe_ref), row_of(pe_ref, False)
    _, p2 = weigh(early_part(xe_ref), x_labels_ref[:EARLY], p, labels, False, True)
    _, p3 = weigh(late_part(xl_ref), x_labels_ref[EARLY:], p, labels, False, True)
    p_ref[...] = p1 + p2 + p3


def early_f_kernel(fe_ref, re_ref, p_in_ref, n_in_ref, p_ref, n_ref, f_labels_ref):
    even = is_even()
    f_labels = label_column(fe_ref, EARLY + LATE)
    f_labels_ref[...] = f_labels
    _, more = weigh(early_part(fe_ref), f_labels[:EARLY], early_part(re_ref), row_of(re_ref, False), False, True)
    p_ref[...] = p_in_ref[...] + jnp.where(even, 0.0, more)
    n_ref[...] = n_in_ref[...] + jnp.where(even, more, 0.0)


def with_late_n(n_ref, ue_ref, ul_ref, xe_ref, xl_ref, pe_ref, ne_ref, n_labels_ref):
    n, labels = late_part(n_ref), n_labels_ref[EARLY:]
    n1, own1 = weigh(n, labels, early_part(ue_ref), row_of(ue_ref, False), True, True)
    n2, own2 = weigh(n, labels, late_part(ul_ref), row_of(ue_ref, True), True, True)
    n3, p1 = weigh(n, labels, early_part(pe_ref), row_of(pe_ref, False), True, True)
    n4, _ = weigh(n, labels, early_part(xe_ref), row_of(xe_ref, False), True, False)
    n5, _ = weigh(n, labels, late_part(xl_ref), row_of(xe_ref, True), True, False)
    return (n1, n2, n3, n4, n5), own1, own2, p1


def with_late_p(p_ref, xe_ref, xl_ref, pe_ref, ne_ref, p_labels_ref):
    p, labels = late_part(p_ref), p_labels_ref[EARLY:]
    p1, n1 = weigh(p, labels, early_part(ne_ref), row_of(ne_ref, False), True, True)
    p2, _ = weigh(p, labels, early_part(xe_ref), row_of(xe_ref, False), True, False)
    p3, _ = weigh(p, labels, late_part(xl_ref), row_of(xe_ref, True), True, False)
    return (p1, p2, p3), n1


def near_kernel(
    pl_ref, nl_ref, ue_ref, ul_ref, xe_ref, xl_ref, ne_ref, pe_ref, p_labels_ref, n_labels_ref,
    own_in_ref, p_in_ref, n_in_ref, own_ref, p_ref, n_ref, p_late_ref, n_late_ref,
):
    upper, lower = is_upper(), is_lower()
    copy_when(upper, own_in_ref, own_ref)
    copy_when(upper, p_in_ref, p_ref)
    copy_when(lower, n_in_ref, n_ref)

    @pl.when(jnp.logical_not(upper))
    def _():
        n, own1, own2, p1 = with_late_n(nl_ref, ue_ref, ul_ref, xe_ref, xl_ref, pe_ref, ne_ref, n_labels_ref)
        own_ref[:, :EARLY] = own_in_ref[:, :EARLY] + own1
        own_ref[:, EARLY:] = own_in_ref[:, EARLY:] + own2
        p_ref[...] = p_in_ref[...] + p1
        n_late_ref[...] = add(*n)

    @pl.when(jnp.logical_not(lower))
    def _():
        p, n1 = with_late_p(pl_ref, xe_ref, xl_ref, pe_ref, ne_ref, p_labels_ref)
        n_ref[...] = n_in_ref[...] + n1
        p_late_ref[...] = add(*p)


def far_kernel(
    w_ref, nl_ref, pl_ref, ue_ref, ul_ref, xe_ref, xl_ref, ne_ref, pe_ref, p_labels_ref, n_labels_ref,
    own_in_ref, p_in_ref, n_in_ref, p_late_ref, n_late_ref, fe_ref, re_ref, rl_ref, f_labels_ref,
    own_ref, p_ref, n_ref,
):
    upper, lower = is_upper(), is_lower()

    @pl.when(upper)
    def _():
        n, own1, own2, p1 = with_late_n(w_ref, ue_ref, ul_ref, xe_ref, xl_ref, pe_ref, ne_ref, n_labels_ref)
        labels = n_labels_ref[EARLY:]
        n6, p2 = weigh(late_part(w_ref), labels, late_part(pl_ref), row_of(pe_ref, True), True, True)
        own_ref[:, :EARLY] = own_in_ref[:, :EARLY] + own1
        own_ref[:, EARLY:] = own_in_ref[:, EARLY:] + own2
        p_ref[:, :EARLY] = p_in_ref[...] + p1
        p_ref[:, EARLY:] = p_late_ref[...] + p2
        n_ref[:, :EARLY] = n_in_ref[...]
        n_ref[:, EARLY:] = add(*n, n6)

    @pl.when(jnp.logical_not(upper))
    def _():
        own_ref[...] = own_in_ref[...]
        p_ref[:, :EARLY] = p_in_ref[...]

    @pl.when(lower)
    def _():
        p, n1 = with_late_p(w_ref, xe_ref, xl_ref, pe_ref, ne_ref, p_labels_ref)
        labels = p_labels_ref[EARLY:]
        p4, n2 = weigh(late_part(w_ref), labels, late_part(nl_ref), row_of(ne_ref, True), True, True)
        p_ref[:, EARLY:] = add(*p, p4)
        n_ref[:, :EARLY] = n_in_ref[...] + n1
        n_ref[:, EARLY:] = n_late_ref[...] + n2

    @pl.when(jnp.logical_not(lower | upper))
    def _():
        labels = p_labels_ref[EARLY:]
        p1, n1 = weigh(late_part(pl_ref), labels, late_part(nl_ref), row_of(ne_ref, True), True, True)
        p_ref[:, EARLY:] = p_late_ref[...] + add(p1)
        n_ref[:, :EARLY] = n_in_ref[...]
        n_ref[:, EARLY:] = n_late_ref[...] + n1

    @pl.when(is_even())
    def _():
        n_ref[:, EARLY:] = n_ref[:, EARLY:] + early_f_late(fe_ref, re_ref, rl_ref, f_labels_ref)


def early_f_late(fe_ref, re_ref, rl_ref, f_labels_ref):
    late = late_part(rl_ref)
    return weigh(early_part(fe_ref), f_labels_ref[:EARLY], late, row_of(re_ref, True), False, True)[1]


def late_f(fl_ref, re_ref, rl_ref, f_labels_ref):
    f, labels = late_part(fl_ref), f_labels_ref[EARLY:]
    _, a = weigh(f, labels, early_part(re_ref), row_of(re_ref, False), False, True)
    _, b = weigh(f, labels, late_part(rl_ref), row_of(re_ref, True), False, True)
    return a, b


def end_n_kernel(fl_ref, re_ref, rl_ref, f_labels_ref, n_in_ref, n_ref):
    copy_when(jnp.logical_not(is_even()), n_in_ref, n_ref)

    @pl.when(is_even())
    def _():
        a, b = late_f(fl_ref, re_ref, rl_ref, f_labels_ref)
        n_ref[...] = n_in_ref[...] + jnp.concatenate([a, b], axis=1)


def end_p_kernel(fe_ref, fl_ref, re_ref, rl_ref, f_labels_ref, p_in_ref, after_ref, p_ref):
    copy_when(is_even(), p_in_ref, p_ref)

    @pl.when(jnp.logical_not(is_even()))
    def _():
        a, b = late_f(fl_ref, re_ref, rl_ref, f_labels_ref)
        c = early_f_late(fe_ref, re_ref, rl_ref, f_labels_ref)
        p_ref[...] = p_in_ref[...] + jnp.concatenate([a, b + c], axis=1)


def sum_kernel(own_ref, more_ref, out_ref):
    out_ref[...] = own_ref[...] + more_ref[...]


def last_kernel(own_ref, more_ref, agreement_ref, log_ref):
    sums = own_ref[...] + more_ref[...]
    agreement = sums[1:2] / sums[0:1]
    log_weight = jnp.log(sums[0:1] * math.exp(-1.0 / TAU))
    for k in range(agreement_ref.shape[0]):
        agreement_ref[k : k + 1, :] = agreement[:, k * LANES : (k + 1) * LANES]
        log_ref[k : k + 1, :] = log_weight[:, k * LANES : (k + 1) * LANES]


def on_device(embeddings, labels):
    n, depth = embeddings.shape
    slabs = depth // LANES
    size = lax.axis_size("blk")
    up = [(i, (i + 2) % size) for i in range(size)]
    down = [(i, (i - 2) % size) for i in range(size)]
    swap = [(i, i ^ 1) for i in range(size)]
    send = lambda array, route: lax.ppermute(array, "blk", route)
    struct = jax.ShapeDtypeStruct
    sums, early_sums = struct((2, n), F32), struct((2, EARLY), F32)
    early, late = struct((HEAD + slabs * EARLY, LANES), BF16), struct((slabs * LATE, LANES), BF16)

    hbm = pl.BlockSpec(memory_space=pltpu.HBM)
    labels = pltpu.with_memory_space_constraint(labels.reshape(n // LANES, LANES), pltpu.HBM)
    ue = call(
        unit_early_kernel,
        early,
        (embeddings, labels),
        "unit_early",
        0.1,
        in_specs=[hbm, hbm],
        scratch=[
            pltpu.VMEM((EARLY, depth), F32),
            pltpu.VMEM((n // LANES, LANES), jnp.int32),
            pltpu.SemaphoreType.DMA((4,)),
            pltpu.SemaphoreType.DMA,
        ],
        limit=52,
    )
    ul = call(
        unit_late_kernel,
        late,
        (embeddings, ue),
        "unit_late",
        0.1,
        in_specs=[hbm, pl.BlockSpec(memory_space=pltpu.VMEM)],
        scratch=[pltpu.VMEM((LATE, depth), F32), pltpu.SemaphoreType.DMA((2,))],
        limit=52,
    )
    pe = send(ue, up)
    ne = send(ue, down)
    xe = send(lax.optimization_barrier((ue, ul))[0], swap)
    xl = send(ul, swap)
    own = call(own_kernel, sums, (ue, ul), "own", 1)
    column, late_sums = struct((n, LANES), F32), struct((2, LATE), F32)
    own, x_labels, copy = call(partner_kernel, (sums, column, late), (ue, ul, xe, xl, own), "with_partner", 1)
    upper = [i for i in range(size) if i % LONG >= LONG - 2]
    far = [(i, (i + 2) % size) for i in upper] + [((i + 2) % size, i) for i in upper]
    late_p = send(copy, [pair for pair in up if pair not in far])
    late_n = send(copy, [pair for pair in down if pair not in far])
    late_w = send(copy, far)

    p_labels = call(labels_kernel, column, (pe, own), "labels", 0.1)
    re = call(pick_early_kernel, early, (pe, ne, p_labels), "pick", 0.1)
    fe = send(re, swap)
    own, p, q, q_labels = call(
        early_kernel,
        (sums, early_sums, early_sums, column),
        (ue, ul, xe, xl, pe, ne, x_labels, own),
        "early",
        2.5,
    )
    p, q, f_labels = call(early_f_kernel, (early_sums, early_sums, column), (fe, re, p, q), "early_f", 0.5)
    fixed = (ue, ul, xe, xl, ne, pe, p_labels, q_labels)
    own, p, q, p_late, q_late = call(
        near_kernel,
        (sums, early_sums, early_sums, late_sums, late_sums),
        (late_p, late_n, *fixed, own, p, q),
        "near",
        1.7,
    )
    rl = call(pick_late_kernel, late, (late_p, late_n, late_w, q), "pick_late", 0.1)
    fl = send(rl, swap)
    own, p, q = call(
        far_kernel,
        (sums, sums, sums),
        (late_w, late_n, late_p, *fixed, own, p, q, p_late, q_late, fe, re, rl, f_labels),
        "far",
        0.2,
    )
    q = call(end_n_kernel, sums, (fl, re, rl, f_labels, q), "end_n", 0.3)
    from_lower = send(q, up)
    p = call(end_p_kernel, sums, (fe, fl, re, rl, f_labels, p, q), "end_p", 0.3)
    from_upper = send(p, down)
    own = call(sum_kernel, sums, (own, from_lower), "sum", 0.001)
    shape = struct((n // LANES, LANES), F32)
    agreement, log_weight = call(last_kernel, (shape, shape), (own, from_upper), "last", 0.01)
    return agreement.reshape(n), log_weight.reshape(n)


def solution(mesh):
    return jax.shard_map(
        on_device,
        mesh=mesh,
        in_specs=(P("blk", None), P("blk")),
        out_specs=(P("blk"), P("blk")),
        check_vma=False,
    )
```
